32 devices in a mesh: patch: 8 (over z, x), grp: 4 (over y, core).
Axes of the slice: x: 2, y: 2, z: 4, core: 2. Of those that a mesh axis runs over, the one named last changes fastest.
Arguments:
- incident: float32 [16, 65536], P(None, ('patch', 'grp')), may hold values from -6 to 6
- self_term: float32 [65536], P(('patch', 'grp')), may hold values from 1 to 3
- near_field: bfloat16 [65536, 2304], P(('patch', 'grp')), may hold values from -0.125 to 0.125
- history: bfloat16 [8, 16, 65536], P(None, None, 'patch'), may hold values from -6 to 6
- ret_values: bfloat16 [8192, 128, 128], P(('patch', 'grp')), may hold values from -0.125 to 0.125
- slot_row: int32 [8192], P(('patch', 'grp')), may hold values from 0 to 15
- slot_col: int32 [8192], P(('patch', 'grp')), may hold values from 0 to 191
- slot_delay: int32 [8192], P(('patch', 'grp')), may hold values from 0 to 7
- live_count: int32 [32], P(('patch', 'grp')), may hold values from 32 to 256, as said below
Outputs:
- current: float32 [16, 65536], P(None, ('patch', 'grp'))
- newest: bfloat16 [16, 65536], P(None, 'patch')
The draws below stay inside these ranges and needn't reach their ends.
Inputs may be any that keep to these rules, and one draw needn't show every extreme that they name: The first live_count[d] slots of shard d are live, the rest ignored; some shard has all 256 slots live.
All inputs are finite; a program needn't handle non-finite values.
Results may differ from the reference program's by a relative error of at most 0.0055.
Values may be sent and summed in bfloat16 or wider, within the bound.
A program may use at most 128 MiB of HBM per device.

```python
import math
import jax
import jax.numpy as jnp
from jax import lax

BLK = 128
WAVES = 16
DELAYS = 8
SWEEPS = 4
RB = 16
SLOTS = 256
UNKNOWNS = 65536
N_PATCH = 8
N_GRP = 4
DEVICES = 32


def draw_live_count(key, part):
    lowest = max(1, SLOTS // 8)
    key_a = jax.random.fold_in(key, 11)
    key_b = jax.random.fold_in(key, 12)
    ranks = jax.random.randint(key_a, (DEVICES,), 0, 64)
    counts = lowest + (SLOTS - lowest) * (ranks * ranks) // 4096
    busiest = jax.random.randint(key_b, (), 0, DEVICES)
    return counts.at[busiest].set(SLOTS).astype(jnp.int32)


def touch_ends(entries, key, smallest, top_value):
    longest = entries.shape.index(max(entries.shape))
    spots = []
    for shift in (0, 1):
        where = [jax.random.randint(jax.random.fold_in(key, axis), (), 0, length) for axis, length in enumerate(entries.shape)]
        where[longest] = (where[longest] + shift) % entries.shape[longest]
        spots.append(tuple(where))
    return entries.at[spots[0]].set(smallest).at[spots[1]].set(top_value)


def shard_levels(own_key, extent, split, smallest, high):
    loudness, own = 1.0, jax.random.fold_in(own_key, 6)
    for dim, parts in split:
        steps = jnp.exp(jax.random.uniform(jax.random.fold_in(own, dim), (parts,), jnp.float32, smallest / len(split), high / len(split)))
        loudness = loudness * jnp.repeat(steps, extent[dim] // parts).reshape([-1 if axis == dim else 1 for axis in range(len(extent))])
    return loudness


def bell_draw(key, dims, scale, most, pieces=(), held_as=jnp.bfloat16):
    entries = jax.random.normal(key, dims, jnp.float32) * scale
    if len(pieces) > 0:
        entries = shard_levels(key, dims, pieces, -0.22, 0.18) * entries
    return jnp.clip(entries, min=-most, max=most).astype(held_as)


def setup_inputs(seed: int = 0) -> dict:
    key_list = jax.random.split(jax.random.key(seed), 10)
    return {
        "incident": bell_draw(key_list[0], (WAVES, UNKNOWNS), 1.0, 6.0, ((1, 32),), jnp.float32),
        "self_term": jnp.clip(jnp.exp(math.log(3.0) - 1.0986123 * jax.random.uniform(key_list[1], (UNKNOWNS,), jnp.float32) ** shard_levels(key_list[1], (UNKNOWNS,), ((0, 32),), -0.2, 0.2)), 1.0, 3.0),
        "near_field": bell_draw(key_list[2], (UNKNOWNS, (RB + 2) * BLK), ((RB + 2) * BLK) ** -0.5, 0.125, ((0, 32),)),
        "history": bell_draw(key_list[3], (DELAYS, WAVES, UNKNOWNS), 1.0, 6.0, ((2, 8),)),
        "ret_values": bell_draw(key_list[4], (DEVICES * SLOTS, BLK, BLK), (BLK * SLOTS // RB) ** -0.5, 0.125, ((0, 32),)),
        "slot_row": touch_ends(jax.random.randint(key_list[5], (DEVICES * SLOTS,), 0, RB), jax.random.fold_in(key_list[5], 1), 0, RB - 1).astype(jnp.int32),
        "slot_col": touch_ends(jax.random.randint(key_list[6], (DEVICES * SLOTS,), 0, 3 * RB * N_GRP), jax.random.fold_in(key_list[6], 1), 0, (3 * RB * N_GRP) - 1).astype(jnp.int32),
        "slot_delay": touch_ends(jax.random.randint(key_list[7], (DEVICES * SLOTS,), 0, DELAYS), jax.random.fold_in(key_list[7], 1), 0, DELAYS - 1).astype(jnp.int32),
        "live_count": draw_live_count(jax.random.fold_in(key_list[9], 71), 0),
    }


def reference(incident, self_term, near_field, history, ret_values, slot_row, slot_col, slot_delay, live_count):
    patch_unk = RB * BLK * N_GRP
    padded = jnp.pad(history, ((0, 0), (0, 0), (patch_unk, patch_unk)))
    values_all = ret_values.reshape(DEVICES, SLOTS, BLK, BLK)
    rows_all = slot_row.reshape(DEVICES, SLOTS)
    cols_all = slot_col.reshape(DEVICES, SLOTS)
    delays_all = slot_delay.reshape(DEVICES, SLOTS)

    def one_device(packed):
        device, values, rows, cols, delays, limit = packed
        patch_id = (device // N_GRP).astype(jnp.int32)
        window = lax.dynamic_slice_in_dim(padded, (patch_id * patch_unk).astype(jnp.int32), 3 * patch_unk, 2)
        window = window.reshape(DELAYS, WAVES, 3 * RB * N_GRP, BLK)
        blocks = window[delays, :, cols, :]
        prods = jnp.einsum("swj,sij->swi", blocks.astype(jnp.float32), values.astype(jnp.float32))
        alive = (jnp.arange(SLOTS, dtype=jnp.int32) < limit).astype(jnp.float32)
        onehot = (rows[None, :] == jnp.arange(RB, dtype=jnp.int32)[:, None]).astype(jnp.float32) * alive[None, :]
        summed = jnp.einsum("rs,swi->wri", onehot, prods, precision=lax.Precision.HIGHEST)
        return summed.reshape(WAVES, RB * BLK)

    retarded = lax.map(one_device, (jnp.arange(DEVICES, dtype=jnp.int32), values_all, rows_all, cols_all, delays_all, live_count))
    retarded = jnp.transpose(retarded, (1, 0, 2)).reshape(WAVES, RB * BLK * DEVICES)
    rhs = incident - retarded
    near_wide = near_field.astype(jnp.float32).reshape(N_PATCH, N_GRP, RB * BLK, (RB + 2) * BLK)
    sweep_in = history[0]
    current = sweep_in.astype(jnp.float32)
    for sweep in range(SWEEPS):
        spread = sweep_in.astype(jnp.float32).reshape(WAVES, N_PATCH, N_GRP, RB * BLK)
        left_edge = jnp.pad(spread[:, :-1, :, -BLK:], ((0, 0), (1, 0), (0, 0), (0, 0)))
        right_edge = jnp.pad(spread[:, 1:, :, :BLK], ((0, 0), (0, 1), (0, 0), (0, 0)))
        extended = jnp.concatenate([left_edge, spread, right_edge], axis=3)
        coupling = jnp.einsum("wpgk,pgik->wpgi", extended, near_wide).reshape(WAVES, RB * BLK * DEVICES)
        current = (rhs - coupling) / self_term[None, :]
        sweep_in = current.astype(jnp.bfloat16)
    return current, sweep_in
```

```python
import functools

import jax
import jax.numpy as jnp
from jax import lax
from jax.experimental import pallas as pl
from jax.experimental.pallas import tpu as pltpu
from jax.sharding import PartitionSpec as P

BLK = 128
SWEEPS = 4
ONLY = 3
TILE = 512
UNROLL = 16
NT = (((1,), (1,)), ((), ()))


def kernel(
    n_patch,
    incident,
    self_term,
    near_hbm,
    hist_hbm,
    ret_hbm,
    row_vec,
    place,
    current,
    newest,
    win,
    blocks,
    near,
    ret,
    prods,
    reduced,
    rhs,
    acc,
    sweep_in,
    edges,
    local_sem,
    x_send,
    x_recv,
    z_send,
    z_recv,
    y_send,
    y_recv,
    c_send,
    c_recv,
    e_send,
    e_recv,
    n_send,
    n_recv,
):
    delays, waves, patch_cols = hist_hbm.shape
    own_cols = incident.shape[1]
    rb = own_cols // BLK
    slots = ret_hbm.shape[0]
    window_blocks = patch_cols // BLK
    half = patch_cols // 2
    fetched = delays - ONLY
    p = lax.axis_index("patch")
    g = lax.axis_index("grp")
    odd = lax.rem(p, 2)
    y = g // 2
    c = lax.rem(g, 2)
    g_core = y * 2 + (1 - c)
    g_plane = (1 - y) * 2 + c
    g_far = (1 - y) * 2 + (1 - c)
    x_peer = p + 1 - 2 * odd
    z_to = p + 2 - 4 * odd
    z_from = p - 2 + 4 * odd
    has_z_to = jnp.logical_and(z_to >= 0, z_to < n_patch)
    has_z_from = jnp.logical_and(z_from >= 0, z_from < n_patch)
    has_left = p > 0
    has_right = p < n_patch - 1
    x_side = 2 - 2 * odd
    z_side = 2 * odd

    def dev(patch, grp):
        return {"patch": patch, "grp": grp}

    def copy(src, dst, send, recv, device):
        return pltpu.make_async_remote_copy(
            src_ref=src,
            dst_ref=dst,
            send_sem=send,
            recv_sem=recv,
            device_id=device,
            device_id_type=pl.DeviceIdType.MESH,
        )

    load_hist = pltpu.make_async_copy(hist_hbm, win.at[1], local_sem.at[0])
    load_near = pltpu.make_async_copy(near_hbm, near, local_sem.at[1])
    load_ret = pltpu.make_async_copy(ret_hbm, ret, local_sem.at[2])
    load_hist.start()
    load_near.start()
    load_ret.start()

    barrier = pltpu.get_barrier_semaphore()

    def greet(patch, grp):
        pl.semaphore_signal(
            barrier, inc=1, device_id=dev(patch, grp), device_id_type=pl.DeviceIdType.MESH
        )

    for grp in (g_core, g_plane, g_far):
        greet(p, grp)
    pl.when(has_left)(lambda: greet(p - 1, g))
    pl.when(has_right)(lambda: greet(p + 1, g))
    pl.when(has_z_to)(lambda: greet(z_to, g))
    pl.when(has_z_from)(lambda: greet(z_from, g))
    met = 3
    for there in (has_left, has_right, has_z_to, has_z_from):
        met = met + there.astype(jnp.int32)
    pl.semaphore_wait(barrier, met)

    mine = pl.ds(pl.multiple_of(c * half, BLK), half)
    other = pl.ds(pl.multiple_of((1 - c) * half, BLK), half)

    def fetched_delay(j):
        return j + y * (delays - ONLY) if j < ONLY else j

    def plane_delay(j):
        return j + (1 - y) * (delays - ONLY)

    def unit(side, delay, cols):
        return win.at[side, delay, :, cols]

    def x_copy(j):
        d = fetched_delay(j)
        return copy(
            hist_hbm.at[d, :, mine], unit(z_side, d, mine), x_send.at[j], x_recv.at[j], dev(x_peer, g)
        )

    def x_arrival(j):
        d = fetched_delay(j)
        ref = unit(x_side, d, mine)
        return copy(ref, ref, x_send.at[j], x_recv.at[j], dev(x_peer, g))

    def z_copy(j):
        d = fetched_delay(j)
        return copy(
            unit(x_side, d, mine), unit(z_side, d, mine), z_send.at[j], z_recv.at[j], dev(z_to, g)
        )

    def z_arrival(j):
        ref = unit(z_side, fetched_delay(j), mine)
        return copy(ref, ref, z_send.at[j], z_recv.at[j], dev(z_from, g))

    def y_copy(kind, j):
        ref = unit((x_side, z_side)[kind], fetched_delay(j), mine)
        return copy(ref, ref, y_send.at[kind, j], y_recv.at[kind, j], dev(p, g_plane))

    def y_arrival(kind, j):
        ref = unit((x_side, z_side)[kind], plane_delay(j), mine)
        return copy(ref, ref, y_send.at[kind, j], y_recv.at[kind, j], dev(p, g_plane))

    def core_delay(i):
        return fetched_delay(i) if i < fetched else plane_delay(i - fetched)

    def core_copy(kind, i):
        ref = unit((x_side, z_side)[kind], core_delay(i), mine)
        return copy(ref, ref, c_send.at[kind, i], c_recv.at[kind, i], dev(p, g_core))

    def core_arrival(kind, i):
        ref = unit((x_side, z_side)[kind], core_delay(i), other)
        return copy(ref, ref, c_send.at[kind, i], c_recv.at[kind, i], dev(p, g_core))

    for j in range(fetched):
        x_copy(j).start()

    @pl.when(jnp.logical_not(has_z_from))
    def _():
        win[z_side] = jnp.zeros(win.shape[1:], win.dtype)
        count = delays * window_blocks
        blocks[pl.ds(z_side * count, count)] = jnp.zeros((count, waves, BLK), blocks.dtype)

    @pl.when(jnp.logical_not(has_left))
    def _():
        for k in range(SWEEPS - 1):
            edges[2 * k] = jnp.zeros((waves, BLK), edges.dtype)

    @pl.when(jnp.logical_not(has_right))
    def _():
        for k in range(SWEEPS - 1):
            edges[2 * k + 1] = jnp.zeros((waves, BLK), edges.dtype)

    def as_blocks(side, delay, part):
        first = part * (window_blocks // 2)
        base = (side * delays + delay) * window_blocks + first

        def some_blocks(step, _):
            for u in range(8):
                b = step * 8 + u
                cols = pl.ds(pl.multiple_of((first + b) * BLK, BLK), BLK)
                blocks[base + b] = win[side, delay, :, cols]
            return 0

        lax.fori_loop(0, window_blocks // 16, some_blocks, 0)

    def own_coupling(state, t):
        rows = pl.ds(pl.multiple_of(t * TILE, TILE), TILE)
        acc[:, rows] = lax.dot_general(
            state, near[rows, BLK : BLK + own_cols], NT, preferred_element_type=jnp.float32
        )

    own = pl.ds(pl.multiple_of(g * own_cols, BLK), own_cols)
    tiles = own_cols // TILE

    def first_coupling(t):
        if t == 0:
            load_hist.wait()
            load_near.wait()
        own_coupling(win[1, 0, :, own], t)

    def on_x(j):
        x_arrival(j).wait_recv()
        pl.when(has_z_to)(lambda: z_copy(j).start())
        if j < ONLY:
            y_copy(0, j).start()
        core_copy(0, j).start()
        as_blocks(x_side, fetched_delay(j), c)

    def on_z(j):
        @pl.when(has_z_from)
        def _():
            z_arrival(j).wait_recv()
            if j < ONLY:
                y_copy(1, j).start()
            core_copy(1, j).start()
            as_blocks(z_side, fetched_delay(j), c)

    def on_y(kind, j):
        def act():
            y_arrival(kind, j).wait_recv()
            core_copy(kind, fetched + j).start()
            as_blocks((x_side, z_side)[kind], plane_delay(j), c)

        act() if kind == 0 else pl.when(has_z_from)(act)

    for j in range(fetched + 4):
        if j < fetched:
            on_x(j)
        if 0 <= j - 1 < fetched:
            on_z(j - 1)
        if 0 <= j - 2 < ONLY:
            on_y(0, j - 2)
        if 0 <= j - 4 < ONLY:
            on_y(1, j - 4)
        if j < tiles:
            first_coupling(j)
        if j < delays:
            as_blocks(1, j, 0)
            as_blocks(1, j, 1)

    load_ret.wait()
    for i in range(delays):
        core_arrival(0, i).wait_recv()
        as_blocks(x_side, core_delay(i), 1 - c)

    @pl.when(has_z_from)
    def _():
        for i in range(delays):
            core_arrival(1, i).wait_recv()
            as_blocks(z_side, core_delay(i), 1 - c)

    def some_slots(step, _):
        for u in range(UNROLL):
            s = step * UNROLL + u
            held = blocks[place[s]]
            prods[pl.ds(pl.multiple_of(s * waves, waves), waves), :] = lax.dot_general(
                held, ret[s], NT, preferred_element_type=jnp.float32
            )
        return 0

    lax.fori_loop(0, slots // UNROLL, some_slots, 0)

    rows_of = lax.broadcasted_iota(jnp.int32, (rb, slots), 0)
    onehot = jnp.where(row_vec[...] == rows_of, 1.0, 0.0).astype(jnp.bfloat16)
    for w in range(waves):
        full = prods[pl.ds(w, slots, stride=waves), :]
        high = full.astype(jnp.bfloat16)
        low = (full - high.astype(jnp.float32)).astype(jnp.bfloat16)
        reduced[pl.ds(w * rb, rb), :] = jnp.dot(
            onehot, high, preferred_element_type=jnp.float32
        ) + jnp.dot(onehot, low, preferred_element_type=jnp.float32)
    for r in range(rb):
        cols = pl.ds(r * BLK, BLK)
        rhs[:, cols] = incident[:, cols] - reduced[pl.ds(r, waves, stride=rb), :]

    def edge_copy(k, to_right):
        if to_right:
            return copy(
                sweep_in.at[k, :, pl.ds(own_cols - BLK, BLK)],
                edges.at[2 * k],
                e_send.at[2 * k],
                e_recv.at[2 * k],
                dev(p + 1, g),
            )
        return copy(
            sweep_in.at[k, :, pl.ds(0, BLK)],
            edges.at[2 * k + 1],
            e_send.at[2 * k + 1],
            e_recv.at[2 * k + 1],
            dev(p - 1, g),
        )

    def edge_arrival(k, from_left):
        i = 2 * k if from_left else 2 * k + 1
        peer = p - 1 if from_left else p + 1
        return copy(edges.at[i], edges.at[i], e_send.at[i], e_recv.at[i], dev(peer, g))

    def newest_copy(i, t):
        part = pl.ds(t * TILE, TILE)
        there = pl.ds(pl.multiple_of(g * own_cols + t * TILE, BLK), TILE)
        return copy(
            sweep_in.at[SWEEPS - 1, :, part],
            newest.at[:, there],
            n_send.at[i, t],
            n_recv.at[i, t],
            dev(p, (g_core, g_plane, g_far)[i]),
        )

    def newest_arrival(i, t):
        source = (g_core, g_plane, g_far)[i]
        ref = newest.at[:, pl.ds(pl.multiple_of(source * own_cols + t * TILE, BLK), TILE)]
        return copy(ref, ref, n_send.at[i, t], n_recv.at[i, t], dev(p, source))

    order = [0, tiles - 1] + list(range(1, tiles - 1))
    for k in range(SWEEPS):
        last = k == SWEEPS - 1
        if k == 0:
            edge_block = pl.multiple_of(g * own_cols, BLK)
            left = win[0, 0, :, pl.ds(pl.multiple_of(edge_block + own_cols - BLK, BLK), BLK)]
            right = win[2, 0, :, pl.ds(edge_block, BLK)]
        else:
            state = sweep_in[k - 1]
            for t in range(tiles):
                own_coupling(state, t)
            pl.when(has_left)(lambda: edge_arrival(k - 1, True).wait_recv())
            pl.when(has_right)(lambda: edge_arrival(k - 1, False).wait_recv())
            left = edges[2 * (k - 1)]
            right = edges[2 * (k - 1) + 1]
        for t in order:
            cols = pl.ds(t * TILE, TILE)
            outer = lax.dot_general(
                left, near[cols, 0:BLK], NT, preferred_element_type=jnp.float32
            ) + lax.dot_general(
                right, near[cols, BLK + own_cols :], NT, preferred_element_type=jnp.float32
            )
            value = (rhs[:, cols] - (acc[:, cols] + outer)) / self_term[:, cols]
            rounded = value.astype(jnp.bfloat16)
            sweep_in[k, :, cols] = rounded
            if last:
                current[:, cols] = value
                for i in range(3):
                    newest_copy(i, t).start()
            elif t == 0:
                pl.when(has_left)(lambda: edge_copy(k, False).start())
            elif t == tiles - 1:
                pl.when(has_right)(lambda: edge_copy(k, True).start())

    newest[:, own] = sweep_in[SWEEPS - 1]

    for j in range(fetched):
        x_copy(j).wait_send()
        pl.when(has_z_to)(lambda: z_copy(j).wait_send())
    for i in range(delays):
        core_copy(0, i).wait_send()
    for j in range(ONLY):
        y_copy(0, j).wait_send()

    @pl.when(has_z_from)
    def _():
        for i in range(delays):
            core_copy(1, i).wait_send()
        for j in range(ONLY):
            y_copy(1, j).wait_send()

    for k in range(SWEEPS - 1):
        pl.when(has_left)(lambda: edge_copy(k, False).wait_send())
        pl.when(has_right)(lambda: edge_copy(k, True).wait_send())
    for t in range(tiles):
        for i in range(3):
            newest_copy(i, t).wait_send()
            newest_arrival(i, t).wait_recv()


def body(
    n_patch,
    incident,
    self_term,
    near_field,
    history,
    ret_values,
    slot_row,
    slot_col,
    slot_delay,
    live_count,
):
    delays, waves, patch_cols = history.shape
    own_cols = incident.shape[1]
    slots = ret_values.shape[0]
    rb = own_cols // BLK
    fetched = delays - ONLY
    tiles = own_cols // TILE
    window_blocks = patch_cols // BLK
    place = (
        slot_col // window_blocks * delays + slot_delay
    ) * window_blocks + slot_col % window_blocks
    live_row = jnp.where(jnp.arange(slots, dtype=jnp.int32) < live_count[0], slot_row, -1)
    dma = pltpu.SemaphoreType.DMA
    vmem = pl.BlockSpec(memory_space=pltpu.VMEM)
    smem = pl.BlockSpec(memory_space=pltpu.SMEM)
    anywhere = pl.BlockSpec(memory_space=pl.ANY)
    return pl.pallas_call(
        functools.partial(kernel, n_patch),
        out_shape=(
            jax.ShapeDtypeStruct((waves, own_cols), jnp.float32),
            jax.ShapeDtypeStruct((waves, patch_cols), jnp.bfloat16),
        ),
        in_specs=[vmem, vmem, anywhere, anywhere, anywhere, vmem, smem],
        out_specs=(vmem, vmem),
        scratch_shapes=[
            pltpu.VMEM((3, delays, waves, patch_cols), jnp.bfloat16),
            pltpu.VMEM((3 * delays * window_blocks, waves, BLK), jnp.bfloat16),
            pltpu.VMEM(near_field.shape, jnp.bfloat16),
            pltpu.VMEM(ret_values.shape, jnp.bfloat16),
            pltpu.VMEM((slots * waves, BLK), jnp.float32),
            pltpu.VMEM((waves * rb, BLK), jnp.float32),
            pltpu.VMEM((waves, own_cols), jnp.float32),
            pltpu.VMEM((waves, own_cols), jnp.float32),
            pltpu.VMEM((SWEEPS, waves, own_cols), jnp.bfloat16),
            pltpu.VMEM((2 * (SWEEPS - 1), waves, BLK), jnp.bfloat16),
            dma((3,)),
            dma((fetched,)),
            dma((fetched,)),
            dma((fetched,)),
            dma((fetched,)),
            dma((2, ONLY)),
            dma((2, ONLY)),
            dma((2, delays)),
            dma((2, delays)),
            dma((2 * (SWEEPS - 1),)),
            dma((2 * (SWEEPS - 1),)),
            dma((3, tiles)),
            dma((3, tiles)),
        ],
        compiler_params=pltpu.CompilerParams(
            collective_id=0, has_side_effects=True, vmem_limit_bytes=48 * 1024 * 1024
        ),
        cost_estimate=pl.CostEstimate(
            flops=2 * waves * own_cols * near_field.shape[1] * SWEEPS,
            bytes_accessed=2 * (near_field.size + ret_values.size + history.size),
            transcendentals=0,
        ),
    )(
        incident,
        self_term.reshape(1, own_cols),
        near_field,
        history,
        ret_values,
        live_row.reshape(1, slots),
        place,
    )


def solution(mesh):
    placed = (
        P(None, ("patch", "grp")),
        P(("patch", "grp")),
        P(("patch", "grp"), None),
        P(None, None, "patch"),
        P(("patch", "grp"), None, None),
        P(("patch", "grp")),
        P(("patch", "grp")),
        P(("patch", "grp")),
        P(("patch", "grp")),
    )
    return jax.shard_map(
        functools.partial(body, mesh.shape["patch"]),
        mesh=mesh,
        in_specs=placed,
        out_specs=(P(None, ("patch", "grp")), P(None, "patch")),
        check_vma=False,
    )
```

```python
import functools

import jax
import jax.numpy as jnp
from jax import lax
from jax.experimental import pallas as pl
from jax.experimental.pallas import tpu as pltpu
from jax.sharding import PartitionSpec as P

BLK = 128
SWEEPS = 4
ONLY = 3
TILE = 512
UNROLL = 8
NT = (((1,), (1,)), ((), ()))


def kernel(
    n_patch,
    incident_hbm,
    self_hbm,
    near_hbm,
    hist_hbm,
    ret_hbm,
    row_hbm,
    col_hbm,
    delay_hbm,
    live_hbm,
    current,
    newest,
    win,
    blocks,
    near,
    ret,
    incident,
    self_term,
    slot_row,
    slot_col,
    slot_delay,
    live,
    picks,
    retarded,
    rhs,
    acc,
    sweep_in,
    edges,
    local_sem,
    x_send,
    x_recv,
    z_send,
    z_recv,
    y_send,
    y_recv,
    c_send,
    c_recv,
    e_send,
    e_recv,
    n_send,
    n_recv,
):
    delays, waves, patch_cols = hist_hbm.shape
    own_cols = incident_hbm.shape[1]
    rb = own_cols // BLK
    slots = ret_hbm.shape[0]
    window_blocks = patch_cols // BLK
    half = patch_cols // 2
    fetched = delays - ONLY
    p = lax.axis_index("patch")
    g = lax.axis_index("grp")
    odd = lax.rem(p, 2)
    y = g // 2
    c = lax.rem(g, 2)
    g_core = y * 2 + (1 - c)
    g_plane = (1 - y) * 2 + c
    g_far = (1 - y) * 2 + (1 - c)
    x_peer = p + 1 - 2 * odd
    z_to = p + 2 - 4 * odd
    z_from = p - 2 + 4 * odd
    has_z_to = jnp.logical_and(z_to >= 0, z_to < n_patch)
    has_z_from = jnp.logical_and(z_from >= 0, z_from < n_patch)
    has_left = p > 0
    has_right = p < n_patch - 1
    x_side = 2 - 2 * odd
    z_side = 2 * odd

    def dev(patch, grp):
        return {"patch": patch, "grp": grp}

    def copy(src, dst, send, recv, device):
        return pltpu.make_async_remote_copy(
            src_ref=src,
            dst_ref=dst,
            send_sem=send,
            recv_sem=recv,
            device_id=device,
            device_id_type=pl.DeviceIdType.MESH,
        )

    load_hist = pltpu.make_async_copy(hist_hbm, win.at[1], local_sem.at[0])
    load_near = pltpu.make_async_copy(near_hbm, near, local_sem.at[1])
    load_ret = pltpu.make_async_copy(ret_hbm, ret, local_sem.at[2])
    load_hist.start()
    load_near.start()
    load_ret.start()
    small = [
        pltpu.make_async_copy(src, dst, local_sem.at[3 + i])
        for i, (src, dst) in enumerate(
            (
                (incident_hbm, incident),
                (self_hbm, self_term),
                (row_hbm, slot_row),
                (col_hbm, slot_col),
                (delay_hbm, slot_delay),
                (live_hbm, live),
            )
        )
    ]
    for one in small:
        one.start()

    barrier = pltpu.get_barrier_semaphore()

    def greet(patch, grp):
        pl.semaphore_signal(
            barrier, inc=1, device_id=dev(patch, grp), device_id_type=pl.DeviceIdType.MESH
        )

    for grp in (g_core, g_plane, g_far):
        greet(p, grp)
    pl.when(has_left)(lambda: greet(p - 1, g))
    pl.when(has_right)(lambda: greet(p + 1, g))
    pl.when(has_z_to)(lambda: greet(z_to, g))
    pl.when(has_z_from)(lambda: greet(z_from, g))
    met = 3
    for there in (has_left, has_right, has_z_to, has_z_from):
        met = met + there.astype(jnp.int32)
    pl.semaphore_wait(barrier, met)

    mine = pl.ds(pl.multiple_of(c * half, BLK), half)
    other = pl.ds(pl.multiple_of((1 - c) * half, BLK), half)

    def fetched_delay(j):
        return j + y * (delays - ONLY) if j < ONLY else j

    def plane_delay(j):
        return j + (1 - y) * (delays - ONLY)

    def unit(side, delay, cols):
        return win.at[side, delay, :, cols]

    def x_copy(j):
        d = fetched_delay(j)
        return copy(
            hist_hbm.at[d, :, mine], unit(z_side, d, mine), x_send.at[j], x_recv.at[j], dev(x_peer, g)
        )

    def x_arrival(j):
        d = fetched_delay(j)
        ref = unit(x_side, d, mine)
        return copy(ref, ref, x_send.at[j], x_recv.at[j], dev(x_peer, g))

    def z_copy(j):
        d = fetched_delay(j)
        return copy(
            unit(x_side, d, mine), unit(z_side, d, mine), z_send.at[j], z_recv.at[j], dev(z_to, g)
        )

    def z_arrival(j):
        ref = unit(z_side, fetched_delay(j), mine)
        return copy(ref, ref, z_send.at[j], z_recv.at[j], dev(z_from, g))

    def y_copy(kind, j):
        ref = unit((x_side, z_side)[kind], fetched_delay(j), mine)
        return copy(ref, ref, y_send.at[kind, j], y_recv.at[kind, j], dev(p, g_plane))

    def y_arrival(kind, j):
        ref = unit((x_side, z_side)[kind], plane_delay(j), mine)
        return copy(ref, ref, y_send.at[kind, j], y_recv.at[kind, j], dev(p, g_plane))

    def core_delay(i):
        return fetched_delay(i) if i < fetched else plane_delay(i - fetched)

    def core_copy(kind, i):
        ref = unit((x_side, z_side)[kind], core_delay(i), mine)
        return copy(ref, ref, c_send.at[kind, i], c_recv.at[kind, i], dev(p, g_core))

    def core_arrival(kind, i):
        ref = unit((x_side, z_side)[kind], core_delay(i), other)
        return copy(ref, ref, c_send.at[kind, i], c_recv.at[kind, i], dev(p, g_core))

    for j in range(fetched):
        x_copy(j).start()

    picks[...] = jnp.zeros(picks.shape, picks.dtype)
    for r in range(rb):
        picks[r, r * waves : (r + 1) * waves, :] = jnp.ones((waves, BLK), picks.dtype)
    retarded[...] = jnp.zeros(retarded.shape, retarded.dtype)

    @pl.when(jnp.logical_not(has_z_from))
    def _():
        win[z_side] = jnp.zeros(win.shape[1:], win.dtype)
        for d in range(delays):
            start = (d * 3 + z_side) * window_blocks
            blocks[pl.ds(start, window_blocks)] = jnp.zeros(
                (window_blocks, waves, BLK), blocks.dtype
            )

    @pl.when(jnp.logical_not(has_left))
    def _():
        for k in range(SWEEPS - 1):
            edges[2 * k] = jnp.zeros((waves, BLK), edges.dtype)

    @pl.when(jnp.logical_not(has_right))
    def _():
        for k in range(SWEEPS - 1):
            edges[2 * k + 1] = jnp.zeros((waves, BLK), edges.dtype)

    def as_blocks(side, delay, part):
        first = part * (window_blocks // 2)
        base = (delay * 3 + side) * window_blocks + first

        def some_blocks(step, _):
            for u in range(8):
                b = step * 8 + u
                cols = pl.ds(pl.multiple_of((first + b) * BLK, BLK), BLK)
                blocks[base + b] = win[side, delay, :, cols]
            return 0

        lax.fori_loop(0, window_blocks // 16, some_blocks, 0)

    def own_coupling(state, t):
        rows = pl.ds(pl.multiple_of(t * TILE, TILE), TILE)
        acc[:, rows] = lax.dot_general(
            state, near[rows, BLK : BLK + own_cols], NT, preferred_element_type=jnp.float32
        )

    own = pl.ds(pl.multiple_of(g * own_cols, BLK), own_cols)
    tiles = own_cols // TILE

    def first_coupling(t):
        if t == 0:
            load_hist.wait()
            load_near.wait()
        own_coupling(win[1, 0, :, own], t)

    def on_x(j):
        x_arrival(j).wait_recv()
        pl.when(has_z_to)(lambda: z_copy(j).start())
        if j < ONLY:
            y_copy(0, j).start()
        core_copy(0, j).start()
        as_blocks(x_side, fetched_delay(j), c)

    def on_z(j):
        @pl.when(has_z_from)
        def _():
            z_arrival(j).wait_recv()
            if j < ONLY:
                y_copy(1, j).start()
            core_copy(1, j).start()
            as_blocks(z_side, fetched_delay(j), c)

    def on_y(kind, j):
        def act():
            y_arrival(kind, j).wait_recv()
            core_copy(kind, fetched + j).start()
            as_blocks((x_side, z_side)[kind], plane_delay(j), c)

        act() if kind == 0 else pl.when(has_z_from)(act)

    for j in range(fetched + 4):
        if j < fetched:
            on_x(j)
        if 0 <= j - 1 < fetched:
            on_z(j - 1)
        if 0 <= j - 2 < ONLY:
            on_y(0, j - 2)
        if 0 <= j - 4 < ONLY:
            on_y(1, j - 4)
        if j < tiles:
            first_coupling(j)
        if j < delays:
            as_blocks(1, j, 0)
            as_blocks(1, j, 1)

    load_ret.wait()
    for one in small:
        one.wait()
    for i in range(delays):
        core_arrival(0, i).wait_recv()
        as_blocks(x_side, core_delay(i), 1 - c)

    @pl.when(has_z_from)
    def _():
        for i in range(delays):
            core_arrival(1, i).wait_recv()
            as_blocks(z_side, core_delay(i), 1 - c)

    limit = live[0]

    def picked(s):
        row = jnp.where(s < limit, slot_row[s], rb)
        held = blocks[slot_delay[s] * (3 * window_blocks) + slot_col[s]]
        return picks[row] * jnp.tile(held, (rb, 1))

    def some_slots(step, _):
        total = retarded[...]
        for u in range(0, UNROLL, 2):
            s = step * UNROLL + u
            total += lax.dot_general(
                jnp.concatenate([picked(s), picked(s + 1)], axis=1),
                jnp.concatenate([ret[s], ret[s + 1]], axis=1),
                NT,
                preferred_element_type=jnp.float32,
            )
        retarded[...] = total
        return 0

    lax.fori_loop(0, slots // UNROLL, some_slots, 0)
    for r in range(rb):
        cols = pl.ds(r * BLK, BLK)
        rhs[:, cols] = incident[:, cols] - retarded[pl.ds(r * waves, waves), :]

    def edge_copy(k, to_right):
        if to_right:
            return copy(
                sweep_in.at[k, :, pl.ds(own_cols - BLK, BLK)],
                edges.at[2 * k],
                e_send.at[2 * k],
                e_recv.at[2 * k],
                dev(p + 1, g),
            )
        return copy(
            sweep_in.at[k, :, pl.ds(0, BLK)],
            edges.at[2 * k + 1],
            e_send.at[2 * k + 1],
            e_recv.at[2 * k + 1],
            dev(p - 1, g),
        )

    def edge_arrival(k, from_left):
        i = 2 * k if from_left else 2 * k + 1
        peer = p - 1 if from_left else p + 1
        return copy(edges.at[i], edges.at[i], e_send.at[i], e_recv.at[i], dev(peer, g))

    def newest_copy(i, t):
        part = pl.ds(t * TILE, TILE)
        there = pl.ds(pl.multiple_of(g * own_cols + t * TILE, BLK), TILE)
        return copy(
            sweep_in.at[SWEEPS - 1, :, part],
            newest.at[:, there],
            n_send.at[i, t],
            n_recv.at[i, t],
            dev(p, (g_core, g_plane, g_far)[i]),
        )

    def newest_arrival(i, t):
        source = (g_core, g_plane, g_far)[i]
        ref = newest.at[:, pl.ds(pl.multiple_of(source * own_cols + t * TILE, BLK), TILE)]
        return copy(ref, ref, n_send.at[i, t], n_recv.at[i, t], dev(p, source))

    order = [0, tiles - 1] + list(range(1, tiles - 1))
    for k in range(SWEEPS):
        last = k == SWEEPS - 1
        if k == 0:
            edge_block = pl.multiple_of(g * own_cols, BLK)
            left = win[0, 0, :, pl.ds(pl.multiple_of(edge_block + own_cols - BLK, BLK), BLK)]
            right = win[2, 0, :, pl.ds(edge_block, BLK)]
        else:
            state = sweep_in[k - 1]
            for t in range(tiles):
                own_coupling(state, t)
            pl.when(has_left)(lambda: edge_arrival(k - 1, True).wait_recv())
            pl.when(has_right)(lambda: edge_arrival(k - 1, False).wait_recv())
            left = edges[2 * (k - 1)]
            right = edges[2 * (k - 1) + 1]
        for t in order:
            cols = pl.ds(t * TILE, TILE)
            outer = lax.dot_general(
                left, near[cols, 0:BLK], NT, preferred_element_type=jnp.float32
            ) + lax.dot_general(
                right, near[cols, BLK + own_cols :], NT, preferred_element_type=jnp.float32
            )
            value = (rhs[:, cols] - (acc[:, cols] + outer)) / self_term[:, cols]
            rounded = value.astype(jnp.bfloat16)
            sweep_in[k, :, cols] = rounded
            if last:
                current[:, cols] = value
                for i in range(3):
                    newest_copy(i, t).start()
            elif t == 0:
                pl.when(has_left)(lambda: edge_copy(k, False).start())
            elif t == tiles - 1:
                pl.when(has_right)(lambda: edge_copy(k, True).start())

    newest[:, own] = sweep_in[SWEEPS - 1]

    for j in range(fetched):
        x_copy(j).wait_send()
        pl.when(has_z_to)(lambda: z_copy(j).wait_send())
    for i in range(delays):
        core_copy(0, i).wait_send()
    for j in range(ONLY):
        y_copy(0, j).wait_send()

    @pl.when(has_z_from)
    def _():
        for i in range(delays):
            core_copy(1, i).wait_send()
        for j in range(ONLY):
            y_copy(1, j).wait_send()

    for k in range(SWEEPS - 1):
        pl.when(has_left)(lambda: edge_copy(k, False).wait_send())
        pl.when(has_right)(lambda: edge_copy(k, True).wait_send())
    for t in range(tiles):
        for i in range(3):
            newest_copy(i, t).wait_send()
            newest_arrival(i, t).wait_recv()


def body(
    n_patch,
    incident,
    self_term,
    near_field,
    history,
    ret_values,
    slot_row,
    slot_col,
    slot_delay,
    live_count,
):
    delays, waves, patch_cols = history.shape
    own_cols = incident.shape[1]
    slots = ret_values.shape[0]
    rb = own_cols // BLK
    fetched = delays - ONLY
    tiles = own_cols // TILE
    window_blocks = patch_cols // BLK
    dma = pltpu.SemaphoreType.DMA
    vmem = pl.BlockSpec(memory_space=pltpu.VMEM)
    in_hbm = pl.BlockSpec(memory_space=pltpu.HBM)
    return pl.pallas_call(
        functools.partial(kernel, n_patch),
        out_shape=(
            jax.ShapeDtypeStruct((waves, own_cols), jnp.float32),
            jax.ShapeDtypeStruct((waves, patch_cols), jnp.bfloat16),
        ),
        in_specs=[in_hbm] * 9,
        out_specs=(vmem, vmem),
        scratch_shapes=[
            pltpu.VMEM((3, delays, waves, patch_cols), jnp.bfloat16),
            pltpu.VMEM((3 * delays * window_blocks, waves, BLK), jnp.bfloat16),
            pltpu.VMEM(near_field.shape, jnp.bfloat16),
            pltpu.VMEM(ret_values.shape, jnp.bfloat16),
            pltpu.VMEM((waves, own_cols), jnp.float32),
            pltpu.VMEM((1, own_cols), jnp.float32),
            pltpu.SMEM((slots,), jnp.int32),
            pltpu.SMEM((slots,), jnp.int32),
            pltpu.SMEM((slots,), jnp.int32),
            pltpu.SMEM((1,), jnp.int32),
            pltpu.VMEM((rb + 1, rb * waves, BLK), jnp.bfloat16),
            pltpu.VMEM((rb * waves, BLK), jnp.float32),
            pltpu.VMEM((waves, own_cols), jnp.float32),
            pltpu.VMEM((waves, own_cols), jnp.float32),
            pltpu.VMEM((SWEEPS, waves, own_cols), jnp.bfloat16),
            pltpu.VMEM((2 * (SWEEPS - 1), waves, BLK), jnp.bfloat16),
            dma((9,)),
            dma((fetched,)),
            dma((fetched,)),
            dma((fetched,)),
            dma((fetched,)),
            dma((2, ONLY)),
            dma((2, ONLY)),
            dma((2, delays)),
            dma((2, delays)),
            dma((2 * (SWEEPS - 1),)),
            dma((2 * (SWEEPS - 1),)),
            dma((3, tiles)),
            dma((3, tiles)),
        ],
        compiler_params=pltpu.CompilerParams(
            collective_id=0, has_side_effects=True, vmem_limit_bytes=56 * 1024 * 1024
        ),
        cost_estimate=pl.CostEstimate(
            flops=2 * waves * own_cols * near_field.shape[1] * SWEEPS,
            bytes_accessed=2 * (near_field.size + ret_values.size + history.size),
            transcendentals=0,
        ),
    )(
        incident,
        self_term.reshape(1, own_cols),
        near_field,
        history,
        ret_values,
        slot_row,
        slot_col,
        slot_delay,
        live_count,
    )


def solution(mesh):
    placed = (
        P(None, ("patch", "grp")),
        P(("patch", "grp")),
        P(("patch", "grp"), None),
        P(None, None, "patch"),
        P(("patch", "grp"), None, None),
        P(("patch", "grp")),
        P(("patch", "grp")),
        P(("patch", "grp")),
        P(("patch", "grp")),
    )
    return jax.shard_map(
        functools.partial(body, mesh.shape["patch"]),
        mesh=mesh,
        in_specs=placed,
        out_specs=(P(None, ("patch", "grp")), P(None, "patch")),
        check_vma=False,
    )
```

```python
import functools

import jax
import jax.numpy as jnp
from jax import lax
from jax.experimental import pallas as pl
from jax.experimental.pallas import tpu as pltpu
from jax.sharding import PartitionSpec as P

BLK = 128
SWEEPS = 4
ONLY = 3
TILE = 512
UNROLL = 8
GROUP = 4
NT = (((1,), (1,)), ((), ()))


def kernel(
    n_patch,
    incident_hbm,
    self_hbm,
    near_hbm,
    hist_hbm,
    ret_hbm,
    row_hbm,
    col_hbm,
    delay_hbm,
    live_hbm,
    current,
    newest,
    win,
    blocks,
    near,
    ret,
    incident,
    self_term,
    slot_row,
    slot_col,
    slot_delay,
    live,
    picks,
    prods,
    retarded,
    rhs,
    acc,
    sweep_in,
    edges,
    local_sem,
    x_send,
    x_recv,
    z_send,
    z_recv,
    y_send,
    y_recv,
    c_send,
    c_recv,
    e_send,
    e_recv,
    n_send,
    n_recv,
):
    delays, waves, patch_cols = hist_hbm.shape
    own_cols = incident_hbm.shape[1]
    rb = own_cols // BLK
    slots = ret_hbm.shape[0]
    window_blocks = patch_cols // BLK
    half = patch_cols // 2
    fetched = delays - ONLY
    p = lax.axis_index("patch")
    g = lax.axis_index("grp")
    odd = lax.rem(p, 2)
    y = g // 2
    c = lax.rem(g, 2)
    g_core = y * 2 + (1 - c)
    g_plane = (1 - y) * 2 + c
    g_far = (1 - y) * 2 + (1 - c)
    x_peer = p + 1 - 2 * odd
    z_to = p + 2 - 4 * odd
    z_from = p - 2 + 4 * odd
    has_z_to = jnp.logical_and(z_to >= 0, z_to < n_patch)
    has_z_from = jnp.logical_and(z_from >= 0, z_from < n_patch)
    has_left = p > 0
    has_right = p < n_patch - 1
    x_side = 2 - 2 * odd
    z_side = 2 * odd

    def dev(patch, grp):
        return {"patch": patch, "grp": grp}

    def copy(src, dst, send, recv, device):
        return pltpu.make_async_remote_copy(
            src_ref=src,
            dst_ref=dst,
            send_sem=send,
            recv_sem=recv,
            device_id=device,
            device_id_type=pl.DeviceIdType.MESH,
        )

    load_hist = pltpu.make_async_copy(hist_hbm, win.at[1], local_sem.at[0])
    load_near = pltpu.make_async_copy(near_hbm, near, local_sem.at[1])
    load_ret = pltpu.make_async_copy(ret_hbm, ret, local_sem.at[2])
    load_hist.start()
    load_near.start()
    load_ret.start()
    small = [
        pltpu.make_async_copy(src, dst, local_sem.at[3 + i])
        for i, (src, dst) in enumerate(
            (
                (incident_hbm, incident),
                (self_hbm, self_term),
                (row_hbm, slot_row),
                (col_hbm, slot_col),
                (delay_hbm, slot_delay),
                (live_hbm, live),
            )
        )
    ]
    for one in small:
        one.start()

    barrier = pltpu.get_barrier_semaphore()

    def greet(patch, grp):
        pl.semaphore_signal(
            barrier, inc=1, device_id=dev(patch, grp), device_id_type=pl.DeviceIdType.MESH
        )

    for grp in (g_core, g_plane, g_far):
        greet(p, grp)
    pl.when(has_left)(lambda: greet(p - 1, g))
    pl.when(has_right)(lambda: greet(p + 1, g))
    pl.when(has_z_to)(lambda: greet(z_to, g))
    pl.when(has_z_from)(lambda: greet(z_from, g))
    met = 3
    for there in (has_left, has_right, has_z_to, has_z_from):
        met = met + there.astype(jnp.int32)
    pl.semaphore_wait(barrier, met)

    mine = pl.ds(pl.multiple_of(c * half, BLK), half)
    other = pl.ds(pl.multiple_of((1 - c) * half, BLK), half)

    def fetched_delay(j):
        return j + y * (delays - ONLY) if j < ONLY else j

    def plane_delay(j):
        return j + (1 - y) * (delays - ONLY)

    def unit(side, delay, cols):
        return win.at[side, delay, :, cols]

    def x_copy(j):
        d = fetched_delay(j)
        return copy(
            hist_hbm.at[d, :, mine], unit(z_side, d, mine), x_send.at[j], x_recv.at[j], dev(x_peer, g)
        )

    def x_arrival(j):
        d = fetched_delay(j)
        ref = unit(x_side, d, mine)
        return copy(ref, ref, x_send.at[j], x_recv.at[j], dev(x_peer, g))

    def z_copy(j):
        d = fetched_delay(j)
        return copy(
            unit(x_side, d, mine), unit(z_side, d, mine), z_send.at[j], z_recv.at[j], dev(z_to, g)
        )

    def z_arrival(j):
        ref = unit(z_side, fetched_delay(j), mine)
        return copy(ref, ref, z_send.at[j], z_recv.at[j], dev(z_from, g))

    def y_copy(kind, j):
        ref = unit((x_side, z_side)[kind], fetched_delay(j), mine)
        return copy(ref, ref, y_send.at[kind, j], y_recv.at[kind, j], dev(p, g_plane))

    def y_arrival(kind, j):
        ref = unit((x_side, z_side)[kind], plane_delay(j), mine)
        return copy(ref, ref, y_send.at[kind, j], y_recv.at[kind, j], dev(p, g_plane))

    def core_delay(i):
        return fetched_delay(i) if i < fetched else plane_delay(i - fetched)

    def core_copy(kind, i):
        ref = unit((x_side, z_side)[kind], core_delay(i), mine)
        return copy(ref, ref, c_send.at[kind, i], c_recv.at[kind, i], dev(p, g_core))

    def core_arrival(kind, i):
        ref = unit((x_side, z_side)[kind], core_delay(i), other)
        return copy(ref, ref, c_send.at[kind, i], c_recv.at[kind, i], dev(p, g_core))

    for j in range(fetched):
        x_copy(j).start()

    wave_of = lax.broadcasted_iota(jnp.int32, (waves, rb * waves), 0)
    lane_of = lax.broadcasted_iota(jnp.int32, (waves, rb * waves), 1)
    for r in range(rb + 1):
        picks[r] = jnp.where(lane_of == wave_of + r * waves, 1.0, 0.0).astype(
            picks.dtype
        ) if r < rb else jnp.zeros((waves, rb * waves), picks.dtype)

    @pl.when(jnp.logical_not(has_z_from))
    def _():
        win[z_side] = jnp.zeros(win.shape[1:], win.dtype)
        for d in range(delays):
            start = (d * 3 + z_side) * window_blocks
            blocks[pl.ds(start, window_blocks)] = jnp.zeros(
                (window_blocks, waves, BLK), blocks.dtype
            )

    @pl.when(jnp.logical_not(has_left))
    def _():
        for k in range(SWEEPS - 1):
            edges[2 * k] = jnp.zeros((waves, BLK), edges.dtype)

    @pl.when(jnp.logical_not(has_right))
    def _():
        for k in range(SWEEPS - 1):
            edges[2 * k + 1] = jnp.zeros((waves, BLK), edges.dtype)

    def as_blocks(side, delay, part):
        first = part * (window_blocks // 2)
        base = (delay * 3 + side) * window_blocks + first

        def some_blocks(step, _):
            for u in range(8):
                b = step * 8 + u
                cols = pl.ds(pl.multiple_of((first + b) * BLK, BLK), BLK)
                blocks[base + b] = win[side, delay, :, cols]
            return 0

        lax.fori_loop(0, window_blocks // 16, some_blocks, 0)

    def own_coupling(state, t):
        rows = pl.ds(pl.multiple_of(t * TILE, TILE), TILE)
        acc[rows, :] = lax.dot_general(
            near[rows, BLK : BLK + own_cols], state, NT, preferred_element_type=jnp.float32
        )

    own = pl.ds(pl.multiple_of(g * own_cols, BLK), own_cols)
    tiles = own_cols // TILE

    def first_coupling(t):
        if t == 0:
            load_hist.wait()
            load_near.wait()
        own_coupling(win[1, 0, :, own], t)

    def on_x(j):
        x_arrival(j).wait_recv()
        pl.when(has_z_to)(lambda: z_copy(j).start())
        if j < ONLY:
            y_copy(0, j).start()
        core_copy(0, j).start()
        as_blocks(x_side, fetched_delay(j), c)

    def on_z(j):
        @pl.when(has_z_from)
        def _():
            z_arrival(j).wait_recv()
            if j < ONLY:
                y_copy(1, j).start()
            core_copy(1, j).start()
            as_blocks(z_side, fetched_delay(j), c)

    def on_y(kind, j):
        def act():
            y_arrival(kind, j).wait_recv()
            core_copy(kind, fetched + j).start()
            as_blocks((x_side, z_side)[kind], plane_delay(j), c)

        act() if kind == 0 else pl.when(has_z_from)(act)

    for j in range(fetched + 4):
        if j < fetched:
            on_x(j)
        if 0 <= j - 1 < fetched:
            on_z(j - 1)
        if 0 <= j - 2 < ONLY:
            on_y(0, j - 2)
        if 0 <= j - 4 < ONLY:
            on_y(1, j - 4)
        if j < tiles:
            first_coupling(j)
        if j < delays:
            as_blocks(1, j, 0)
            as_blocks(1, j, 1)

    load_ret.wait()
    for one in small:
        one.wait()
    for i in range(delays):
        core_arrival(0, i).wait_recv()
        as_blocks(x_side, core_delay(i), 1 - c)

    @pl.when(has_z_from)
    def _():
        for i in range(delays):
            core_arrival(1, i).wait_recv()
            as_blocks(z_side, core_delay(i), 1 - c)

    limit = live[0]
    none = jnp.zeros((waves, BLK), jnp.bfloat16)

    def some_slots(step, _):
        strips = []
        for first in range(0, UNROLL, GROUP):
            held = []
            for u in range(GROUP):
                s = step * UNROLL + first + u
                block = blocks[slot_delay[s] * (3 * window_blocks) + slot_col[s]]
                held.append(
                    jnp.concatenate([block if v == u else none for v in range(GROUP)], axis=1)
                )
            begin = step * UNROLL + first
            strips.append(
                lax.dot_general(
                    jnp.concatenate([ret[begin + u] for u in range(GROUP)], axis=1),
                    jnp.concatenate(held, axis=0),
                    NT,
                    preferred_element_type=jnp.float32,
                )
            )
        full = jnp.concatenate(strips, axis=1)
        high = full.astype(jnp.bfloat16)
        low = (full - high.astype(jnp.float32)).astype(jnp.bfloat16)
        prods[step, 0:BLK, :] = high
        prods[step, BLK:, :] = low
        return 0

    lax.fori_loop(0, slots // UNROLL, some_slots, 0, unroll=2)
    total = jnp.zeros((2 * BLK, rb * waves), jnp.float32)
    for step in range(0, slots // UNROLL, 4):
        chosen = []
        for u in range(4 * UNROLL):
            s = step * UNROLL + u
            chosen.append(picks[jnp.where(s < limit, slot_row[s], rb)])
        total += jnp.dot(
            jnp.concatenate([prods[step + i] for i in range(4)], axis=1),
            jnp.concatenate(chosen, axis=0),
            preferred_element_type=jnp.float32,
        )
    retarded[...] = jnp.transpose(total[0:BLK] + total[BLK:])
    for r in range(rb):
        cols = pl.ds(r * BLK, BLK)
        rhs[:, cols] = incident[:, cols] - retarded[pl.ds(r * waves, waves), :]

    def edge_copy(k, to_right):
        if to_right:
            return copy(
                sweep_in.at[k, :, pl.ds(own_cols - BLK, BLK)],
                edges.at[2 * k],
                e_send.at[2 * k],
                e_recv.at[2 * k],
                dev(p + 1, g),
            )
        return copy(
            sweep_in.at[k, :, pl.ds(0, BLK)],
            edges.at[2 * k + 1],
            e_send.at[2 * k + 1],
            e_recv.at[2 * k + 1],
            dev(p - 1, g),
        )

    def edge_arrival(k, from_left):
        i = 2 * k if from_left else 2 * k + 1
        peer = p - 1 if from_left else p + 1
        return copy(edges.at[i], edges.at[i], e_send.at[i], e_recv.at[i], dev(peer, g))

    def newest_copy(i, t):
        part = pl.ds(t * TILE, TILE)
        there = pl.ds(pl.multiple_of(g * own_cols + t * TILE, BLK), TILE)
        return copy(
            sweep_in.at[SWEEPS - 1, :, part],
            newest.at[:, there],
            n_send.at[i, t],
            n_recv.at[i, t],
            dev(p, (g_core, g_plane, g_far)[i]),
        )

    def newest_arrival(i, t):
        source = (g_core, g_plane, g_far)[i]
        ref = newest.at[:, pl.ds(pl.multiple_of(source * own_cols + t * TILE, BLK), TILE)]
        return copy(ref, ref, n_send.at[i, t], n_recv.at[i, t], dev(p, source))

    order = [0, tiles - 1] + list(range(1, tiles - 1))
    for k in range(SWEEPS):
        last = k == SWEEPS - 1
        if k == 0:
            edge_block = pl.multiple_of(g * own_cols, BLK)
            left = win[0, 0, :, pl.ds(pl.multiple_of(edge_block + own_cols - BLK, BLK), BLK)]
            right = win[2, 0, :, pl.ds(edge_block, BLK)]
        else:
            state = sweep_in[k - 1]
            for t in range(tiles):
                own_coupling(state, t)
            pl.when(has_left)(lambda: edge_arrival(k - 1, True).wait_recv())
            pl.when(has_right)(lambda: edge_arrival(k - 1, False).wait_recv())
            left = edges[2 * (k - 1)]
            right = edges[2 * (k - 1) + 1]
        ends = jnp.concatenate([left, right], axis=1)
        for t in order:
            cols = pl.ds(t * TILE, TILE)
            outer = lax.dot_general(
                jnp.concatenate([near[cols, 0:BLK], near[cols, BLK + own_cols :]], axis=1),
                ends,
                NT,
                preferred_element_type=jnp.float32,
            )
            coupling = jnp.transpose(acc[cols, :] + outer)
            value = (rhs[:, cols] - coupling) / self_term[:, cols]
            rounded = value.astype(jnp.bfloat16)
            sweep_in[k, :, cols] = rounded
            if last:
                current[:, cols] = value
                for i in range(3):
                    newest_copy(i, t).start()
            elif t == 0:
                pl.when(has_left)(lambda: edge_copy(k, False).start())
            elif t == tiles - 1:
                pl.when(has_right)(lambda: edge_copy(k, True).start())

    newest[:, own] = sweep_in[SWEEPS - 1]

    for j in range(fetched):
        x_copy(j).wait_send()
        pl.when(has_z_to)(lambda: z_copy(j).wait_send())
    for i in range(delays):
        core_copy(0, i).wait_send()
    for j in range(ONLY):
        y_copy(0, j).wait_send()

    @pl.when(has_z_from)
    def _():
        for i in range(delays):
            core_copy(1, i).wait_send()
        for j in range(ONLY):
            y_copy(1, j).wait_send()

    for k in range(SWEEPS - 1):
        pl.when(has_left)(lambda: edge_copy(k, False).wait_send())
        pl.when(has_right)(lambda: edge_copy(k, True).wait_send())
    for t in range(tiles):
        for i in range(3):
            newest_copy(i, t).wait_send()
            newest_arrival(i, t).wait_recv()


def body(
    n_patch,
    incident,
    self_term,
    near_field,
    history,
    ret_values,
    slot_row,
    slot_col,
    slot_delay,
    live_count,
):
    delays, waves, patch_cols = history.shape
    own_cols = incident.shape[1]
    slots = ret_values.shape[0]
    rb = own_cols // BLK
    fetched = delays - ONLY
    tiles = own_cols // TILE
    window_blocks = patch_cols // BLK
    dma = pltpu.SemaphoreType.DMA
    vmem = pl.BlockSpec(memory_space=pltpu.VMEM)
    in_hbm = pl.BlockSpec(memory_space=pltpu.HBM)
    return pl.pallas_call(
        functools.partial(kernel, n_patch),
        out_shape=(
            jax.ShapeDtypeStruct((waves, own_cols), jnp.float32),
            jax.ShapeDtypeStruct((waves, patch_cols), jnp.bfloat16),
        ),
        in_specs=[in_hbm] * 9,
        out_specs=(vmem, vmem),
        scratch_shapes=[
            pltpu.VMEM((3, delays, waves, patch_cols), jnp.bfloat16),
            pltpu.VMEM((3 * delays * window_blocks, waves, BLK), jnp.bfloat16),
            pltpu.VMEM(near_field.shape, jnp.bfloat16),
            pltpu.VMEM(ret_values.shape, jnp.bfloat16),
            pltpu.VMEM((waves, own_cols), jnp.float32),
            pltpu.VMEM((1, own_cols), jnp.float32),
            pltpu.SMEM((slots,), jnp.int32),
            pltpu.SMEM((slots,), jnp.int32),
            pltpu.SMEM((slots,), jnp.int32),
            pltpu.SMEM((1,), jnp.int32),
            pltpu.VMEM((rb + 1, waves, rb * waves), jnp.bfloat16),
            pltpu.VMEM((slots // UNROLL, 2 * BLK, UNROLL * waves), jnp.bfloat16),
            pltpu.VMEM((rb * waves, BLK), jnp.float32),
            pltpu.VMEM((waves, own_cols), jnp.float32),
            pltpu.VMEM((own_cols, waves), jnp.float32),
            pltpu.VMEM((SWEEPS, waves, own_cols), jnp.bfloat16),
            pltpu.VMEM((2 * (SWEEPS - 1), waves, BLK), jnp.bfloat16),
            dma((9,)),
            dma((fetched,)),
            dma((fetched,)),
            dma((fetched,)),
            dma((fetched,)),
            dma((2, ONLY)),
            dma((2, ONLY)),
            dma((2, delays)),
            dma((2, delays)),
            dma((2 * (SWEEPS - 1),)),
            dma((2 * (SWEEPS - 1),)),
            dma((3, tiles)),
            dma((3, tiles)),
        ],
        compiler_params=pltpu.CompilerParams(
            collective_id=0, has_side_effects=True, vmem_limit_bytes=56 * 1024 * 1024
        ),
        cost_estimate=pl.CostEstimate(
            flops=2 * waves * own_cols * near_field.shape[1] * SWEEPS,
            bytes_accessed=2 * (near_field.size + ret_values.size + history.size),
            transcendentals=0,
        ),
    )(
        incident,
        self_term.reshape(1, own_cols),
        near_field,
        history,
        ret_values,
        slot_row,
        slot_col,
        slot_delay,
        live_count,
    )


def solution(mesh):
    placed = (
        P(None, ("patch", "grp")),
        P(("patch", "grp")),
        P(("patch", "grp"), None),
        P(None, None, "patch"),
        P(("patch", "grp"), None, None),
        P(("patch", "grp")),
        P(("patch", "grp")),
        P(("patch", "grp")),
        P(("patch", "grp")),
    )
    return jax.shard_map(
        functools.partial(body, mesh.shape["patch"]),
        mesh=mesh,
        in_specs=placed,
        out_specs=(P(None, ("patch", "grp")), P(None, "patch")),
        check_vma=False,
    )
```

```python
import functools

import jax
import jax.numpy as jnp
from jax import lax
from jax.experimental import pallas as pl
from jax.experimental.pallas import tpu as pltpu
from jax.sharding import PartitionSpec as P

BLK = 128
SWEEPS = 4
ONLY = 2
TILE = 512
UNROLL = 8
GROUP = 4
NT = (((1,), (1,)), ((), ()))


def kernel(
    n_patch,
    incident_hbm,
    self_hbm,
    near_hbm,
    hist_hbm,
    ret_hbm,
    row_hbm,
    col_hbm,
    delay_hbm,
    live_hbm,
    current_hbm,
    newest,
    win,
    blocks,
    near,
    ret,
    incident,
    self_term,
    slot_row,
    slot_col,
    slot_delay,
    live,
    picks,
    prods,
    retarded,
    rhs,
    current,
    acc,
    sweep_in,
    edges,
    local_sem,
    x_send,
    x_recv,
    z_send,
    z_recv,
    y_send,
    y_recv,
    c_send,
    c_recv,
    e_send,
    e_recv,
    n_send,
    n_recv,
    out_sem,
):
    delays, waves, patch_cols = hist_hbm.shape
    own_cols = incident_hbm.shape[1]
    rb = own_cols // BLK
    slots = ret_hbm.shape[0]
    window_blocks = patch_cols // BLK
    half = patch_cols // 2
    fetched = delays - ONLY
    p = lax.axis_index("patch")
    g = lax.axis_index("grp")
    odd = lax.rem(p, 2)
    y = g // 2
    c = lax.rem(g, 2)
    g_core = y * 2 + (1 - c)
    g_plane = (1 - y) * 2 + c
    g_far = (1 - y) * 2 + (1 - c)
    x_peer = p + 1 - 2 * odd
    z_to = p + 2 - 4 * odd
    z_from = p - 2 + 4 * odd
    has_z_to = jnp.logical_and(z_to >= 0, z_to < n_patch)
    has_z_from = jnp.logical_and(z_from >= 0, z_from < n_patch)
    has_left = p > 0
    has_right = p < n_patch - 1
    x_side = 2 - 2 * odd
    z_side = 2 * odd

    def dev(patch, grp):
        return {"patch": patch, "grp": grp}

    def copy(src, dst, send, recv, device):
        return pltpu.make_async_remote_copy(
            src_ref=src,
            dst_ref=dst,
            send_sem=send,
            recv_sem=recv,
            device_id=device,
            device_id_type=pl.DeviceIdType.MESH,
        )

    load_hist = pltpu.make_async_copy(hist_hbm, win.at[1], local_sem.at[0])
    load_near = pltpu.make_async_copy(near_hbm, near, local_sem.at[1])
    load_ret = pltpu.make_async_copy(ret_hbm, ret, local_sem.at[2])
    load_hist.start()
    load_near.start()
    load_ret.start()
    small = [
        pltpu.make_async_copy(src, dst, local_sem.at[3 + i])
        for i, (src, dst) in enumerate(
            (
                (incident_hbm, incident),
                (self_hbm, self_term),
                (row_hbm, slot_row),
                (col_hbm, slot_col),
                (delay_hbm, slot_delay),
                (live_hbm, live),
            )
        )
    ]
    for one in small:
        one.start()

    barrier = pltpu.get_barrier_semaphore()

    def greet(patch, grp):
        pl.semaphore_signal(
            barrier, inc=1, device_id=dev(patch, grp), device_id_type=pl.DeviceIdType.MESH
        )

    for grp in (g_core, g_plane, g_far):
        greet(p, grp)
    pl.when(has_left)(lambda: greet(p - 1, g))
    pl.when(has_right)(lambda: greet(p + 1, g))
    pl.when(has_z_to)(lambda: greet(z_to, g))
    pl.when(has_z_from)(lambda: greet(z_from, g))
    met = 3
    for there in (has_left, has_right, has_z_to, has_z_from):
        met = met + there.astype(jnp.int32)
    pl.semaphore_wait(barrier, met)

    mine = pl.ds(pl.multiple_of(c * half, BLK), half)
    other = pl.ds(pl.multiple_of((1 - c) * half, BLK), half)

    def fetched_delay(j):
        return j + y * (delays - ONLY) if j < ONLY else j

    def plane_delay(j):
        return j + (1 - y) * (delays - ONLY)

    def unit(side, delay, cols):
        return win.at[side, delay, :, cols]

    def x_copy(j):
        d = fetched_delay(j)
        return copy(
            hist_hbm.at[d, :, mine], unit(z_side, d, mine), x_send.at[j], x_recv.at[j], dev(x_peer, g)
        )

    def x_arrival(j):
        d = fetched_delay(j)
        ref = unit(x_side, d, mine)
        return copy(ref, ref, x_send.at[j], x_recv.at[j], dev(x_peer, g))

    def z_copy(j):
        d = fetched_delay(j)
        return copy(
            unit(x_side, d, mine), unit(z_side, d, mine), z_send.at[j], z_recv.at[j], dev(z_to, g)
        )

    def z_arrival(j):
        ref = unit(z_side, fetched_delay(j), mine)
        return copy(ref, ref, z_send.at[j], z_recv.at[j], dev(z_from, g))

    def y_copy(kind, j):
        ref = unit((x_side, z_side)[kind], fetched_delay(j), mine)
        return copy(ref, ref, y_send.at[kind, j], y_recv.at[kind, j], dev(p, g_plane))

    def y_arrival(kind, j):
        ref = unit((x_side, z_side)[kind], plane_delay(j), mine)
        return copy(ref, ref, y_send.at[kind, j], y_recv.at[kind, j], dev(p, g_plane))

    def core_delay(i):
        return fetched_delay(i) if i < fetched else plane_delay(i - fetched)

    def core_copy(kind, i):
        ref = unit((x_side, z_side)[kind], core_delay(i), mine)
        return copy(ref, ref, c_send.at[kind, i], c_recv.at[kind, i], dev(p, g_core))

    def core_arrival(kind, i):
        ref = unit((x_side, z_side)[kind], core_delay(i), other)
        return copy(ref, ref, c_send.at[kind, i], c_recv.at[kind, i], dev(p, g_core))

    for j in range(fetched):
        x_copy(j).start()

    wave_of = lax.broadcasted_iota(jnp.int32, (waves, rb * waves), 0)
    lane_of = lax.broadcasted_iota(jnp.int32, (waves, rb * waves), 1)
    for r in range(rb + 1):
        picks[r] = jnp.where(lane_of == wave_of + r * waves, 1.0, 0.0).astype(
            picks.dtype
        ) if r < rb else jnp.zeros((waves, rb * waves), picks.dtype)

    @pl.when(jnp.logical_not(has_z_from))
    def _():
        win[z_side] = jnp.zeros(win.shape[1:], win.dtype)
        for d in range(delays):
            start = (d * 3 + z_side) * window_blocks
            blocks[pl.ds(start, window_blocks)] = jnp.zeros(
                (window_blocks, waves, BLK), blocks.dtype
            )

    @pl.when(jnp.logical_not(has_left))
    def _():
        for k in range(SWEEPS - 1):
            edges[2 * k] = jnp.zeros((waves, BLK), edges.dtype)

    @pl.when(jnp.logical_not(has_right))
    def _():
        for k in range(SWEEPS - 1):
            edges[2 * k + 1] = jnp.zeros((waves, BLK), edges.dtype)

    def as_blocks(side, delay, part):
        first = part * (window_blocks // 2)
        base = (delay * 3 + side) * window_blocks + first

        def some_blocks(step, _):
            for u in range(8):
                b = step * 8 + u
                cols = pl.ds(pl.multiple_of((first + b) * BLK, BLK), BLK)
                blocks[base + b] = win[side, delay, :, cols]
            return 0

        lax.fori_loop(0, window_blocks // 16, some_blocks, 0)

    def own_coupling(state, t):
        rows = pl.ds(pl.multiple_of(t * TILE, TILE), TILE)
        acc[rows, :] = lax.dot_general(
            near[rows, BLK : BLK + own_cols], state, NT, preferred_element_type=jnp.float32
        )

    own = pl.ds(pl.multiple_of(g * own_cols, BLK), own_cols)
    tiles = own_cols // TILE

    def first_coupling(t):
        if t == 0:
            load_hist.wait()
            load_near.wait()
        own_coupling(win[1, 0, :, own], t)

    def on_x(j):
        x_arrival(j).wait_recv()
        pl.when(has_z_to)(lambda: z_copy(j).start())
        if j < ONLY:
            y_copy(0, j).start()
        core_copy(0, j).start()
        as_blocks(x_side, fetched_delay(j), c)

    def on_z(j):
        @pl.when(has_z_from)
        def _():
            z_arrival(j).wait_recv()
            if j < ONLY:
                y_copy(1, j).start()
            core_copy(1, j).start()
            as_blocks(z_side, fetched_delay(j), c)

    def on_y(kind, j):
        def act():
            y_arrival(kind, j).wait_recv()
            core_copy(kind, fetched + j).start()
            as_blocks((x_side, z_side)[kind], plane_delay(j), c)

        act() if kind == 0 else pl.when(has_z_from)(act)

    for j in range(fetched + 4):
        if j < fetched:
            on_x(j)
        if 0 <= j - 1 < fetched:
            on_z(j - 1)
        if 0 <= j - 2 < ONLY:
            on_y(0, j - 2)
        if 0 <= j - 4 < ONLY:
            on_y(1, j - 4)
        if j < tiles:
            first_coupling(j)
        if j < delays:
            as_blocks(1, j, 0)
            as_blocks(1, j, 1)

    load_ret.wait()
    for one in small:
        one.wait()
    for i in range(delays):
        core_arrival(0, i).wait_recv()
        as_blocks(x_side, core_delay(i), 1 - c)

    @pl.when(has_z_from)
    def _():
        for i in range(delays):
            core_arrival(1, i).wait_recv()
            as_blocks(z_side, core_delay(i), 1 - c)

    limit = live[0]
    none = jnp.zeros((waves, BLK), jnp.bfloat16)

    def some_slots(step, _):
        strips = []
        for first in range(0, UNROLL, GROUP):
            held = []
            for u in range(GROUP):
                s = step * UNROLL + first + u
                block = blocks[slot_delay[s] * (3 * window_blocks) + slot_col[s]]
                held.append(
                    jnp.concatenate([block if v == u else none for v in range(GROUP)], axis=1)
                )
            begin = step * UNROLL + first
            strips.append(
                lax.dot_general(
                    jnp.concatenate([ret[begin + u] for u in range(GROUP)], axis=1),
                    jnp.concatenate(held, axis=0),
                    NT,
                    preferred_element_type=jnp.float32,
                )
            )
        full = jnp.concatenate(strips, axis=1)
        high = full.astype(jnp.bfloat16)
        low = (full - high.astype(jnp.float32)).astype(jnp.bfloat16)
        prods[step, 0:BLK, :] = high
        prods[step, BLK:, :] = low
        return 0

    lax.fori_loop(0, slots // UNROLL, some_slots, 0, unroll=2)
    total = jnp.zeros((2 * BLK, rb * waves), jnp.float32)
    for step in range(0, slots // UNROLL, 4):
        chosen = []
        for u in range(4 * UNROLL):
            s = step * UNROLL + u
            chosen.append(picks[jnp.where(s < limit, slot_row[s], rb)])
        total += jnp.dot(
            jnp.concatenate([prods[step + i] for i in range(4)], axis=1),
            jnp.concatenate(chosen, axis=0),
            preferred_element_type=jnp.float32,
        )
    retarded[...] = jnp.transpose(total[0:BLK] + total[BLK:])
    for r in range(rb):
        cols = pl.ds(r * BLK, BLK)
        rhs[:, cols] = incident[:, cols] - retarded[pl.ds(r * waves, waves), :]

    def edge_copy(k, to_right):
        if to_right:
            return copy(
                sweep_in.at[k, :, pl.ds(own_cols - BLK, BLK)],
                edges.at[2 * k],
                e_send.at[2 * k],
                e_recv.at[2 * k],
                dev(p + 1, g),
            )
        return copy(
            sweep_in.at[k, :, pl.ds(0, BLK)],
            edges.at[2 * k + 1],
            e_send.at[2 * k + 1],
            e_recv.at[2 * k + 1],
            dev(p - 1, g),
        )

    def edge_arrival(k, from_left):
        i = 2 * k if from_left else 2 * k + 1
        peer = p - 1 if from_left else p + 1
        return copy(edges.at[i], edges.at[i], e_send.at[i], e_recv.at[i], dev(peer, g))

    peers = (g_core, g_plane, g_far)

    def newest_copy(i, t):
        part = pl.ds(t * TILE, TILE)
        return copy(
            sweep_in.at[SWEEPS - 1, :, part],
            newest.at[g, :, part],
            n_send.at[i, t],
            n_recv.at[i, t],
            dev(p, peers[i]),
        )

    def newest_arrival(i, t):
        ref = newest.at[peers[i], :, pl.ds(t * TILE, TILE)]
        return copy(ref, ref, n_send.at[i, t], n_recv.at[i, t], dev(p, peers[i]))

    def out_copies(t):
        part = pl.ds(t * TILE, TILE)
        return (
            pltpu.make_async_copy(current.at[:, part], current_hbm.at[:, part], out_sem.at[0, t]),
            pltpu.make_async_copy(
                sweep_in.at[SWEEPS - 1, :, part], newest.at[g, :, part], out_sem.at[1, t]
            ),
        )

    order = [0, tiles - 1] + list(range(1, tiles - 1))
    for k in range(SWEEPS):
        last = k == SWEEPS - 1
        if k == 0:
            edge_block = pl.multiple_of(g * own_cols, BLK)
            left = win[0, 0, :, pl.ds(pl.multiple_of(edge_block + own_cols - BLK, BLK), BLK)]
            right = win[2, 0, :, pl.ds(edge_block, BLK)]
        else:
            state = sweep_in[k - 1]
            for t in range(tiles):
                own_coupling(state, t)
            pl.when(has_left)(lambda: edge_arrival(k - 1, True).wait_recv())
            pl.when(has_right)(lambda: edge_arrival(k - 1, False).wait_recv())
            left = edges[2 * (k - 1)]
            right = edges[2 * (k - 1) + 1]
        ends = jnp.concatenate([left, right], axis=1)
        for t in order:
            cols = pl.ds(t * TILE, TILE)
            outer = lax.dot_general(
                jnp.concatenate([near[cols, 0:BLK], near[cols, BLK + own_cols :]], axis=1),
                ends,
                NT,
                preferred_element_type=jnp.float32,
            )
            coupling = jnp.transpose(acc[cols, :] + outer)
            value = rhs[:, cols] - coupling
            rounded = (value / self_term[:, cols]).astype(jnp.bfloat16)
            sweep_in[k, :, cols] = rounded
            if last:
                current[:, cols] = value
                for i in range(3):
                    newest_copy(i, t).start()
                for one in out_copies(t):
                    one.start()
            elif t == 0:
                pl.when(has_left)(lambda: edge_copy(k, False).start())
            elif t == tiles - 1:
                pl.when(has_right)(lambda: edge_copy(k, True).start())

    for j in range(fetched):
        x_copy(j).wait_send()
        pl.when(has_z_to)(lambda: z_copy(j).wait_send())
    for i in range(delays):
        core_copy(0, i).wait_send()
    for j in range(ONLY):
        y_copy(0, j).wait_send()

    @pl.when(has_z_from)
    def _():
        for i in range(delays):
            core_copy(1, i).wait_send()
        for j in range(ONLY):
            y_copy(1, j).wait_send()

    for k in range(SWEEPS - 1):
        pl.when(has_left)(lambda: edge_copy(k, False).wait_send())
        pl.when(has_right)(lambda: edge_copy(k, True).wait_send())
    for t in range(tiles):
        for one in out_copies(t):
            one.wait()
        for i in range(3):
            newest_copy(i, t).wait_send()
            newest_arrival(i, t).wait_recv()


def body(
    n_patch,
    incident,
    self_term,
    near_field,
    history,
    ret_values,
    slot_row,
    slot_col,
    slot_delay,
    live_count,
):
    delays, waves, patch_cols = history.shape
    own_cols = incident.shape[1]
    slots = ret_values.shape[0]
    rb = own_cols // BLK
    fetched = delays - ONLY
    tiles = own_cols // TILE
    window_blocks = patch_cols // BLK
    dma = pltpu.SemaphoreType.DMA
    in_hbm = pl.BlockSpec(memory_space=pltpu.HBM)
    numerator, newest = pl.pallas_call(
        functools.partial(kernel, n_patch),
        out_shape=(
            jax.ShapeDtypeStruct((waves, own_cols), jnp.float32),
            jax.ShapeDtypeStruct((patch_cols // own_cols, waves, own_cols), jnp.bfloat16),
        ),
        in_specs=[in_hbm] * 9,
        out_specs=(in_hbm, in_hbm),
        scratch_shapes=[
            pltpu.VMEM((3, delays, waves, patch_cols), jnp.bfloat16),
            pltpu.VMEM((3 * delays * window_blocks, waves, BLK), jnp.bfloat16),
            pltpu.VMEM(near_field.shape, jnp.bfloat16),
            pltpu.VMEM(ret_values.shape, jnp.bfloat16),
            pltpu.VMEM((waves, own_cols), jnp.float32),
            pltpu.VMEM((1, own_cols), jnp.float32),
            pltpu.SMEM((slots,), jnp.int32),
            pltpu.SMEM((slots,), jnp.int32),
            pltpu.SMEM((slots,), jnp.int32),
            pltpu.SMEM((1,), jnp.int32),
            pltpu.VMEM((rb + 1, waves, rb * waves), jnp.bfloat16),
            pltpu.VMEM((slots // UNROLL, 2 * BLK, UNROLL * waves), jnp.bfloat16),
            pltpu.VMEM((rb * waves, BLK), jnp.float32),
            pltpu.VMEM((waves, own_cols), jnp.float32),
            pltpu.VMEM((waves, own_cols), jnp.float32),
            pltpu.VMEM((own_cols, waves), jnp.float32),
            pltpu.VMEM((SWEEPS, waves, own_cols), jnp.bfloat16),
            pltpu.VMEM((2 * (SWEEPS - 1), waves, BLK), jnp.bfloat16),
            dma((9,)),
            dma((fetched,)),
            dma((fetched,)),
            dma((fetched,)),
            dma((fetched,)),
            dma((2, ONLY)),
            dma((2, ONLY)),
            dma((2, delays)),
            dma((2, delays)),
            dma((2 * (SWEEPS - 1),)),
            dma((2 * (SWEEPS - 1),)),
            dma((3, tiles)),
            dma((3, tiles)),
            dma((2, tiles)),
        ],
        compiler_params=pltpu.CompilerParams(
            collective_id=0, has_side_effects=True, vmem_limit_bytes=56 * 1024 * 1024
        ),
        cost_estimate=pl.CostEstimate(
            flops=2 * waves * own_cols * near_field.shape[1] * SWEEPS,
            bytes_accessed=2 * (near_field.size + ret_values.size + history.size),
            transcendentals=0,
        ),
    )(
        incident,
        self_term.reshape(1, own_cols),
        near_field,
        history,
        ret_values,
        slot_row,
        slot_col,
        slot_delay,
        live_count,
    )
    return numerator / self_term[None, :], newest.transpose(1, 0, 2).reshape(waves, patch_cols)


def solution(mesh):
    placed = (
        P(None, ("patch", "grp")),
        P(("patch", "grp")),
        P(("patch", "grp"), None),
        P(None, None, "patch"),
        P(("patch", "grp"), None, None),
        P(("patch", "grp")),
        P(("patch", "grp")),
        P(("patch", "grp")),
        P(("patch", "grp")),
    )
    return jax.shard_map(
        functools.partial(body, mesh.shape["patch"]),
        mesh=mesh,
        in_specs=placed,
        out_specs=(P(None, ("patch", "grp")), P(None, "patch")),
        check_vma=False,
    )
```

```python
import functools

import jax
import jax.numpy as jnp
from jax import lax
from jax.experimental import pallas as pl
from jax.experimental.pallas import tpu as pltpu
from jax.sharding import PartitionSpec as P

BLK = 128
SWEEPS = 4
PARTS = 2
ONLY = 5
TILE = 512
UNROLL = 8
GROUP = 4
NT = (((1,), (1,)), ((), ()))


def kernel(
    n_patch,
    incident_hbm,
    self_hbm,
    near_hbm,
    hist_hbm,
    ret_hbm,
    row_hbm,
    col_hbm,
    delay_hbm,
    live_hbm,
    current_hbm,
    newest,
    win,
    blocks,
    near,
    ret,
    incident,
    self_term,
    slot_row,
    slot_col,
    slot_delay,
    live,
    picks,
    prods,
    retarded,
    rhs,
    current,
    acc,
    sweep_in,
    edges,
    local_sem,
    x_send,
    x_recv,
    z_send,
    z_recv,
    y_send,
    y_recv,
    c_send,
    c_recv,
    e_send,
    e_recv,
    n_send,
    n_recv,
    out_sem,
):
    delays, waves, patch_cols = hist_hbm.shape
    own_cols = incident_hbm.shape[1]
    rb = own_cols // BLK
    slots = ret_hbm.shape[0]
    window_blocks = patch_cols // BLK
    half = patch_cols // 2
    units = delays * PARTS
    unit_cols = half // PARTS
    fetched = units - ONLY
    p = lax.axis_index("patch")
    g = lax.axis_index("grp")
    odd = lax.rem(p, 2)
    y = g // 2
    c = lax.rem(g, 2)
    g_core = y * 2 + (1 - c)
    g_plane = (1 - y) * 2 + c
    g_far = (1 - y) * 2 + (1 - c)
    x_peer = p + 1 - 2 * odd
    z_to = p + 2 - 4 * odd
    z_from = p - 2 + 4 * odd
    has_z_to = jnp.logical_and(z_to >= 0, z_to < n_patch)
    has_z_from = jnp.logical_and(z_from >= 0, z_from < n_patch)
    has_left = p > 0
    has_right = p < n_patch - 1
    x_side = 2 - 2 * odd
    z_side = 2 * odd

    def dev(patch, grp):
        return {"patch": patch, "grp": grp}

    def copy(src, dst, send, recv, device):
        return pltpu.make_async_remote_copy(
            src_ref=src,
            dst_ref=dst,
            send_sem=send,
            recv_sem=recv,
            device_id=device,
            device_id_type=pl.DeviceIdType.MESH,
        )

    load_hist = pltpu.make_async_copy(hist_hbm, win.at[1], local_sem.at[0])
    load_near = pltpu.make_async_copy(near_hbm, near, local_sem.at[1])
    load_ret = pltpu.make_async_copy(ret_hbm, ret, local_sem.at[2])
    load_hist.start()
    load_near.start()
    load_ret.start()
    small = [
        pltpu.make_async_copy(src, dst, local_sem.at[3 + i])
        for i, (src, dst) in enumerate(
            (
                (incident_hbm, incident),
                (self_hbm, self_term),
                (row_hbm, slot_row),
                (col_hbm, slot_col),
                (delay_hbm, slot_delay),
                (live_hbm, live),
            )
        )
    ]
    for one in small:
        one.start()

    barrier = pltpu.get_barrier_semaphore()

    def greet(patch, grp):
        pl.semaphore_signal(
            barrier, inc=1, device_id=dev(patch, grp), device_id_type=pl.DeviceIdType.MESH
        )

    for grp in (g_core, g_plane, g_far):
        greet(p, grp)
    pl.when(has_left)(lambda: greet(p - 1, g))
    pl.when(has_right)(lambda: greet(p + 1, g))
    pl.when(has_z_to)(lambda: greet(z_to, g))
    pl.when(has_z_from)(lambda: greet(z_from, g))
    met = 3
    for there in (has_left, has_right, has_z_to, has_z_from):
        met = met + there.astype(jnp.int32)
    pl.semaphore_wait(barrier, met)

    def fetched_unit(j):
        return j + y * (units - ONLY) if j < ONLY else j

    def plane_unit(j):
        return j + (1 - y) * (units - ONLY)

    def columns(core, i):
        start = core * half + lax.rem(i, PARTS) * unit_cols
        return pl.ds(pl.multiple_of(start, BLK), unit_cols)

    def unit(side, i, core=c):
        return win.at[side, i // PARTS, :, columns(core, i)]

    def x_copy(j):
        i = fetched_unit(j)
        src = hist_hbm.at[i // PARTS, :, columns(c, i)]
        return copy(src, unit(z_side, i), x_send.at[j], x_recv.at[j], dev(x_peer, g))

    def x_arrival(j):
        ref = unit(x_side, fetched_unit(j))
        return copy(ref, ref, x_send.at[j], x_recv.at[j], dev(x_peer, g))

    def z_copy(j):
        i = fetched_unit(j)
        return copy(unit(x_side, i), unit(z_side, i), z_send.at[j], z_recv.at[j], dev(z_to, g))

    def z_arrival(j):
        ref = unit(z_side, fetched_unit(j))
        return copy(ref, ref, z_send.at[j], z_recv.at[j], dev(z_from, g))

    def y_copy(kind, j):
        ref = unit((x_side, z_side)[kind], fetched_unit(j))
        return copy(ref, ref, y_send.at[kind, j], y_recv.at[kind, j], dev(p, g_plane))

    def y_arrival(kind, j):
        ref = unit((x_side, z_side)[kind], plane_unit(j))
        return copy(ref, ref, y_send.at[kind, j], y_recv.at[kind, j], dev(p, g_plane))

    def core_unit(i):
        return fetched_unit(i) if i < fetched else plane_unit(i - fetched)

    def core_copy(kind, i):
        ref = unit((x_side, z_side)[kind], core_unit(i))
        return copy(ref, ref, c_send.at[kind, i], c_recv.at[kind, i], dev(p, g_core))

    def core_arrival(kind, i):
        ref = unit((x_side, z_side)[kind], core_unit(i), 1 - c)
        return copy(ref, ref, c_send.at[kind, i], c_recv.at[kind, i], dev(p, g_core))

    for j in range(fetched):
        x_copy(j).start()

    wave_of = lax.broadcasted_iota(jnp.int32, (waves, rb * waves), 0)
    lane_of = lax.broadcasted_iota(jnp.int32, (waves, rb * waves), 1)
    for r in range(rb + 1):
        picks[r] = jnp.where(lane_of == wave_of + r * waves, 1.0, 0.0).astype(
            picks.dtype
        ) if r < rb else jnp.zeros((waves, rb * waves), picks.dtype)

    @pl.when(jnp.logical_not(has_z_from))
    def _():
        win[z_side] = jnp.zeros(win.shape[1:], win.dtype)
        for d in range(delays):
            start = (d * 3 + z_side) * window_blocks
            blocks[pl.ds(start, window_blocks)] = jnp.zeros(
                (window_blocks, waves, BLK), blocks.dtype
            )

    @pl.when(jnp.logical_not(has_left))
    def _():
        for k in range(SWEEPS - 1):
            edges[2 * k] = jnp.zeros((waves, BLK), edges.dtype)

    @pl.when(jnp.logical_not(has_right))
    def _():
        for k in range(SWEEPS - 1):
            edges[2 * k + 1] = jnp.zeros((waves, BLK), edges.dtype)

    unit_blocks = unit_cols // BLK

    def as_blocks(side, i, core):
        i = jnp.int32(i)
        first = (core * PARTS + lax.rem(i, PARTS)) * unit_blocks
        delay = i // PARTS
        base = (delay * 3 + side) * window_blocks + first

        def some_blocks(step, _):
            for u in range(8):
                b = step * 8 + u
                cols = pl.ds(pl.multiple_of((first + b) * BLK, BLK), BLK)
                blocks[base + b] = win[side, delay, :, cols]
            return 0

        lax.fori_loop(0, unit_blocks // 8, some_blocks, 0)

    def own_coupling(state, t):
        rows = pl.ds(pl.multiple_of(t * TILE, TILE), TILE)
        acc[rows, :] = lax.dot_general(
            near[rows, BLK : BLK + own_cols], state, NT, preferred_element_type=jnp.float32
        )

    own = pl.ds(pl.multiple_of(g * own_cols, BLK), own_cols)
    tiles = own_cols // TILE

    def first_coupling(t):
        if t == 0:
            load_hist.wait()
            load_near.wait()
        own_coupling(win[1, 0, :, own], t)

    def on_x(j):
        x_arrival(j).wait_recv()
        pl.when(has_z_to)(lambda: z_copy(j).start())
        if j < ONLY:
            y_copy(0, j).start()
        core_copy(0, j).start()
        as_blocks(x_side, fetched_unit(j), c)

    def on_z(j):
        @pl.when(has_z_from)
        def _():
            z_arrival(j).wait_recv()
            if j < ONLY:
                y_copy(1, j).start()
            core_copy(1, j).start()
            as_blocks(z_side, fetched_unit(j), c)

    def on_y(kind, j):
        def act():
            y_arrival(kind, j).wait_recv()
            core_copy(kind, fetched + j).start()
            as_blocks((x_side, z_side)[kind], plane_unit(j), c)

        act() if kind == 0 else pl.when(has_z_from)(act)

    def on_core(kind, i):
        def act():
            core_arrival(kind, i).wait_recv()
            as_blocks((x_side, z_side)[kind], core_unit(i), 1 - c)

        act() if kind == 0 else pl.when(has_z_from)(act)

    for j in range(fetched + 3):
        if j < fetched:
            on_x(j)
        if 0 <= j - 1 < fetched:
            on_z(j - 1)
        if j >= 3 and j % 2 == 1 and (j - 3) // 2 < ONLY:
            on_y(0, (j - 3) // 2)
        if j >= 4 and j % 2 == 0 and (j - 4) // 2 < ONLY:
            on_y(1, (j - 4) // 2)
        if 0 <= j - 2 < fetched:
            on_core(0, j - 2)
        if 0 <= j - 3 < fetched:
            on_core(1, j - 3)
        if j < tiles:
            first_coupling(j)
        if j < delays:
            for i in range(PARTS * j, PARTS * (j + 1)):
                as_blocks(1, i, 0)
                as_blocks(1, i, 1)
    for j in range(ONLY):
        on_core(0, fetched + j)
        on_core(1, fetched + j)

    load_ret.wait()
    for one in small:
        one.wait()
    limit = live[0]
    none = jnp.zeros((waves, BLK), jnp.bfloat16)

    def some_slots(step, _):
        strips = []
        for first in range(0, UNROLL, GROUP):
            held = []
            for u in range(GROUP):
                s = step * UNROLL + first + u
                block = blocks[slot_delay[s] * (3 * window_blocks) + slot_col[s]]
                held.append(
                    jnp.concatenate([block if v == u else none for v in range(GROUP)], axis=1)
                )
            begin = step * UNROLL + first
            strips.append(
                lax.dot_general(
                    jnp.concatenate([ret[begin + u] for u in range(GROUP)], axis=1),
                    jnp.concatenate(held, axis=0),
                    NT,
                    preferred_element_type=jnp.float32,
                )
            )
        full = jnp.concatenate(strips, axis=1)
        high = full.astype(jnp.bfloat16)
        low = (full - high.astype(jnp.float32)).astype(jnp.bfloat16)
        prods[step, 0:BLK, :] = high
        prods[step, BLK:, :] = low
        return 0

    lax.fori_loop(0, slots // UNROLL, some_slots, 0, unroll=4)
    total = jnp.zeros((2 * BLK, rb * waves), jnp.float32)
    for step in range(0, slots // UNROLL, 4):
        chosen = []
        for u in range(4 * UNROLL):
            s = step * UNROLL + u
            chosen.append(picks[jnp.where(s < limit, slot_row[s], rb)])
        total += jnp.dot(
            jnp.concatenate([prods[step + i] for i in range(4)], axis=1),
            jnp.concatenate(chosen, axis=0),
            preferred_element_type=jnp.float32,
        )
    retarded[...] = jnp.transpose(total[0:BLK] + total[BLK:])
    for r in range(rb):
        cols = pl.ds(r * BLK, BLK)
        rhs[:, cols] = incident[:, cols] - retarded[pl.ds(r * waves, waves), :]

    def edge_copy(k, to_right):
        if to_right:
            return copy(
                sweep_in.at[k, :, pl.ds(own_cols - BLK, BLK)],
                edges.at[2 * k],
                e_send.at[2 * k],
                e_recv.at[2 * k],
                dev(p + 1, g),
            )
        return copy(
            sweep_in.at[k, :, pl.ds(0, BLK)],
            edges.at[2 * k + 1],
            e_send.at[2 * k + 1],
            e_recv.at[2 * k + 1],
            dev(p - 1, g),
        )

    def edge_arrival(k, from_left):
        i = 2 * k if from_left else 2 * k + 1
        peer = p - 1 if from_left else p + 1
        return copy(edges.at[i], edges.at[i], e_send.at[i], e_recv.at[i], dev(peer, g))

    peers = (g_core, g_plane, g_far)

    def newest_copy(i, t):
        part = pl.ds(t * TILE, TILE)
        return copy(
            sweep_in.at[SWEEPS - 1, :, part],
            newest.at[g, :, part],
            n_send.at[i, t],
            n_recv.at[i, t],
            dev(p, peers[i]),
        )

    def newest_arrival(i, t):
        ref = newest.at[peers[i], :, pl.ds(t * TILE, TILE)]
        return copy(ref, ref, n_send.at[i, t], n_recv.at[i, t], dev(p, peers[i]))

    def out_copies(t):
        part = pl.ds(t * TILE, TILE)
        return (
            pltpu.make_async_copy(current.at[:, part], current_hbm.at[:, part], out_sem.at[0, t]),
            pltpu.make_async_copy(
                sweep_in.at[SWEEPS - 1, :, part], newest.at[g, :, part], out_sem.at[1, t]
            ),
        )

    order = [0, tiles - 1] + list(range(1, tiles - 1))
    for k in range(SWEEPS):
        last = k == SWEEPS - 1
        if k == 0:
            edge_block = pl.multiple_of(g * own_cols, BLK)
            left = win[0, 0, :, pl.ds(pl.multiple_of(edge_block + own_cols - BLK, BLK), BLK)]
            right = win[2, 0, :, pl.ds(edge_block, BLK)]
        else:
            state = sweep_in[k - 1]
            for t in range(tiles):
                own_coupling(state, t)
            pl.when(has_left)(lambda: edge_arrival(k - 1, True).wait_recv())
            pl.when(has_right)(lambda: edge_arrival(k - 1, False).wait_recv())
            left = edges[2 * (k - 1)]
            right = edges[2 * (k - 1) + 1]
        ends = jnp.concatenate([left, right], axis=1)
        for t in order:
            cols = pl.ds(t * TILE, TILE)
            outer = lax.dot_general(
                jnp.concatenate([near[cols, 0:BLK], near[cols, BLK + own_cols :]], axis=1),
                ends,
                NT,
                preferred_element_type=jnp.float32,
            )
            coupling = jnp.transpose(acc[cols, :] + outer)
            value = rhs[:, cols] - coupling
            rounded = (value / self_term[:, cols]).astype(jnp.bfloat16)
            sweep_in[k, :, cols] = rounded
            if last:
                current[:, cols] = value
                for i in range(3):
                    newest_copy(i, t).start()
                for one in out_copies(t):
                    one.start()
            elif t == 0:
                pl.when(has_left)(lambda: edge_copy(k, False).start())
            elif t == tiles - 1:
                pl.when(has_right)(lambda: edge_copy(k, True).start())

    for j in range(fetched):
        x_copy(j).wait_send()
        pl.when(has_z_to)(lambda: z_copy(j).wait_send())
    for i in range(units):
        core_copy(0, i).wait_send()
    for j in range(ONLY):
        y_copy(0, j).wait_send()

    @pl.when(has_z_from)
    def _():
        for i in range(units):
            core_copy(1, i).wait_send()
        for j in range(ONLY):
            y_copy(1, j).wait_send()

    for k in range(SWEEPS - 1):
        pl.when(has_left)(lambda: edge_copy(k, False).wait_send())
        pl.when(has_right)(lambda: edge_copy(k, True).wait_send())
    for t in range(tiles):
        for one in out_copies(t):
            one.wait()
        for i in range(3):
            newest_copy(i, t).wait_send()
            newest_arrival(i, t).wait_recv()


def body(
    n_patch,
    incident,
    self_term,
    near_field,
    history,
    ret_values,
    slot_row,
    slot_col,
    slot_delay,
    live_count,
):
    delays, waves, patch_cols = history.shape
    own_cols = incident.shape[1]
    slots = ret_values.shape[0]
    rb = own_cols // BLK
    units = delays * PARTS
    fetched = units - ONLY
    tiles = own_cols // TILE
    window_blocks = patch_cols // BLK
    dma = pltpu.SemaphoreType.DMA
    in_hbm = pl.BlockSpec(memory_space=pltpu.HBM)
    numerator, newest = pl.pallas_call(
        functools.partial(kernel, n_patch),
        out_shape=(
            jax.ShapeDtypeStruct((waves, own_cols), jnp.float32),
            jax.ShapeDtypeStruct((patch_cols // own_cols, waves, own_cols), jnp.bfloat16),
        ),
        in_specs=[in_hbm] * 9,
        out_specs=(in_hbm, in_hbm),
        scratch_shapes=[
            pltpu.VMEM((3, delays, waves, patch_cols), jnp.bfloat16),
            pltpu.VMEM((3 * delays * window_blocks, waves, BLK), jnp.bfloat16),
            pltpu.VMEM(near_field.shape, jnp.bfloat16),
            pltpu.VMEM(ret_values.shape, jnp.bfloat16),
            pltpu.VMEM((waves, own_cols), jnp.float32),
            pltpu.VMEM((1, own_cols), jnp.float32),
            pltpu.SMEM((slots,), jnp.int32),
            pltpu.SMEM((slots,), jnp.int32),
            pltpu.SMEM((slots,), jnp.int32),
            pltpu.SMEM((1,), jnp.int32),
            pltpu.VMEM((rb + 1, waves, rb * waves), jnp.bfloat16),
            pltpu.VMEM((slots // UNROLL, 2 * BLK, UNROLL * waves), jnp.bfloat16),
            pltpu.VMEM((rb * waves, BLK), jnp.float32),
            pltpu.VMEM((waves, own_cols), jnp.float32),
            pltpu.VMEM((waves, own_cols), jnp.float32),
            pltpu.VMEM((own_cols, waves), jnp.float32),
            pltpu.VMEM((SWEEPS, waves, own_cols), jnp.bfloat16),
            pltpu.VMEM((2 * (SWEEPS - 1), waves, BLK), jnp.bfloat16),
            dma((9,)),
            dma((fetched,)),
            dma((fetched,)),
            dma((fetched,)),
            dma((fetched,)),
            dma((2, ONLY)),
            dma((2, ONLY)),
            dma((2, units)),
            dma((2, units)),
            dma((2 * (SWEEPS - 1),)),
            dma((2 * (SWEEPS - 1),)),
            dma((3, tiles)),
            dma((3, tiles)),
            dma((2, tiles)),
        ],
        compiler_params=pltpu.CompilerParams(
            collective_id=0, has_side_effects=True, vmem_limit_bytes=56 * 1024 * 1024
        ),
        cost_estimate=pl.CostEstimate(
            flops=2 * waves * own_cols * near_field.shape[1] * SWEEPS,
            bytes_accessed=2 * (near_field.size + ret_values.size + history.size),
            transcendentals=0,
        ),
    )(
        incident,
        self_term.reshape(1, own_cols),
        near_field,
        history,
        ret_values,
        slot_row,
        slot_col,
        slot_delay,
        live_count,
    )
    return numerator / self_term[None, :], newest.transpose(1, 0, 2).reshape(waves, patch_cols)


def solution(mesh):
    placed = (
        P(None, ("patch", "grp")),
        P(("patch", "grp")),
        P(("patch", "grp"), None),
        P(None, None, "patch"),
        P(("patch", "grp"), None, None),
        P(("patch", "grp")),
        P(("patch", "grp")),
        P(("patch", "grp")),
        P(("patch", "grp")),
    )
    return jax.shard_map(
        functools.partial(body, mesh.shape["patch"]),
        mesh=mesh,
        in_specs=placed,
        out_specs=(P(None, ("patch", "grp")), P(None, "patch")),
        check_vma=False,
    )
```
